512 devices in a mesh: gx: 64 (over y, x, core), ta: 8 (over z).
Axes of the slice: x: 4, y: 8, z: 8, core: 2. Of those that a mesh axis runs over, the one named last changes fastest.
Arguments:
- field: bfloat16 [20, 8, 64, 128, 128], P(None, 'ta', 'gx'), may hold values from -6 to 6
- spectral_weight: float32 [2, 24, 576, 4, 20, 20], P(None, 'ta', 'gx'), may hold values from -6 to 6
- local_weight: float32 [20, 20], replicated, may hold values from -1.25 to 1.25
- cotangent: bfloat16 [20, 8, 64, 128, 128], P(None, 'ta', 'gx'), may hold values from -6 to 6
Outputs:
- layer_out: float32 [20, 8, 64, 128, 128], P(None, 'ta', 'gx')
- grad_field: float32 [20, 8, 64, 128, 128], P(None, 'ta', 'gx')
- grad_spectral: float32 [2, 24, 576, 4, 20, 20], P(None, 'ta', 'gx')
The draws below stay inside these ranges and needn't reach their ends.
All inputs are finite; a program needn't handle non-finite values.
Results may differ from the reference program's by a relative error of at most 0.0003.
Values sent between devices are 32-bit elements; how exact they have to be, the bound alone decides.
A program may use at most 64 MiB of HBM per device.

```python
import math
import jax
import jax.numpy as jnp
from jax import lax

C = 20
MODES = 12
KT = 4
KF = 24
Y = 128
Z = 128
X = 64
T_SIZE = 8
P_SIZE = 576


def levels(own_key, dims, pieces, low, high):
    loudness, own = 1.0, jax.random.fold_in(own_key, 6)
    for axis_at, shards_of in pieces:
        steps = jnp.exp(jax.random.uniform(jax.random.fold_in(own, axis_at), (shards_of,), jnp.float32, low / len(pieces), high / len(pieces)))
        loudness = loudness * jnp.repeat(steps, dims[axis_at] // shards_of).reshape([-1 if axis == axis_at else 1 for axis in range(len(dims))])
    return loudness


def noise(rng, extent, scale, limit, shards=(), kind=jnp.bfloat16):
    array = scale * jax.random.normal(rng, extent, jnp.float32)
    if shards:
        array = array * levels(rng, extent, shards, -0.22, 0.18)
    return jnp.clip(array, -limit, limit).astype(kind)


def setup_inputs(seed: int = 0) -> dict:
    key_list = jax.random.split(jax.random.key(seed), 5)
    return {
        "field": noise(key_list[0], (C, T_SIZE, X, Y, Z), 1.0, 6.0, ((1, 8), (2, 64))),
        "spectral_weight": noise(key_list[1], (2, KF, P_SIZE, KT, C, C), 1.0, 6.0, ((1, 8), (2, 64)), jnp.float32),
        "local_weight": noise(key_list[2], (C, C), C ** -0.5, 1.25, (), jnp.float32),
        "cotangent": noise(key_list[3], (C, T_SIZE, X, Y, Z), 1.0, 6.0, ((1, 8), (2, 64))),
    }


HIGHEST = lax.Precision.HIGHEST

def contract(formula, left, right):
    return jnp.einsum(formula, left, right, precision=HIGHEST)

def kept_frequencies():
    position = jnp.arange(KF, dtype=jnp.int32)
    return jnp.where(position < MODES, position, position - KF)

def phase_tables(period, positions, frequencies):
    phase_turns = positions[:, None] * frequencies[None, :] % period
    angles = phase_turns.astype(jnp.float32) * (2.0 * math.pi / period)
    return (jnp.cos(angles), jnp.sin(angles))

def time_weights():
    return jnp.where(jnp.arange(KT, dtype=jnp.int32) == 0, 1.0, 2.0).astype(jnp.float32)

def all_tables(total_steps, cells_x, cells_y, cells_z):
    frequencies = kept_frequencies()
    tables_x = phase_tables(cells_x, jnp.arange(cells_x, dtype=jnp.int32), frequencies)
    tables_y = phase_tables(cells_y, jnp.arange(cells_y, dtype=jnp.int32), frequencies)
    tables_z = phase_tables(cells_z, jnp.arange(cells_z, dtype=jnp.int32), frequencies)
    tables_t = phase_tables(total_steps, jnp.arange(total_steps, dtype=jnp.int32), jnp.arange(KT, dtype=jnp.int32))
    return (tables_t, tables_x, tables_y, tables_z)

def analyse(field, tables, factor):
    (cos_t, sin_t), (cos_x, sin_x), (cos_y, sin_y), (cos_z, sin_z) = tables
    real_z = contract('ctxyz,zk->ctxyk', field, cos_z)
    imag_z = -contract('ctxyz,zk->ctxyk', field, sin_z)
    real_y = contract('ctxyk,yj->ctxjk', real_z, cos_y) + contract('ctxyk,yj->ctxjk', imag_z, sin_y)
    imag_y = contract('ctxyk,yj->ctxjk', imag_z, cos_y) - contract('ctxyk,yj->ctxjk', real_z, sin_y)
    real_x = contract('ctxjk,xi->ctijk', real_y, cos_x) + contract('ctxjk,xi->ctijk', imag_y, sin_x)
    imag_x = contract('ctxjk,xi->ctijk', imag_y, cos_x) - contract('ctxjk,xi->ctijk', real_y, sin_x)
    real_t = contract('ctijk,tm->cijkm', real_x, cos_t) + contract('ctijk,tm->cijkm', imag_x, sin_t)
    imag_t = contract('ctijk,tm->cijkm', imag_x, cos_t) - contract('ctijk,tm->cijkm', real_x, sin_t)
    chans = field.shape[0]
    return ((real_t * factor).reshape(chans, KF, KF * KF, KT), (imag_t * factor).reshape(chans, KF, KF * KF, KT))

def synthesise(real_part, imag_part, tables, factor):
    (cos_t, sin_t), (cos_x, sin_x), (cos_y, sin_y), (cos_z, sin_z) = tables
    chans = real_part.shape[0]
    weights = time_weights()
    real_part = (real_part * weights).reshape(chans, KF, KF, KF, KT)
    imag_part = (imag_part * weights).reshape(chans, KF, KF, KF, KT)
    real_t = contract('cijkm,tm->ctijk', real_part, cos_t) - contract('cijkm,tm->ctijk', imag_part, sin_t)
    imag_t = contract('cijkm,tm->ctijk', real_part, sin_t) + contract('cijkm,tm->ctijk', imag_part, cos_t)
    real_x = contract('ctijk,xi->ctxjk', real_t, cos_x) - contract('ctijk,xi->ctxjk', imag_t, sin_x)
    imag_x = contract('ctijk,xi->ctxjk', real_t, sin_x) + contract('ctijk,xi->ctxjk', imag_t, cos_x)
    real_y = contract('ctxjk,yj->ctxyk', real_x, cos_y) - contract('ctxjk,yj->ctxyk', imag_x, sin_y)
    imag_y = contract('ctxjk,yj->ctxyk', real_x, sin_y) + contract('ctxjk,yj->ctxyk', imag_x, cos_y)
    result = contract('ctxyk,zk->ctxyz', real_y, cos_z) - contract('ctxyk,zk->ctxyz', imag_y, sin_z)
    return result * factor

def gelu_parts(pre_act):
    normal_cdf = 0.5 * (1.0 + lax.erf(pre_act * (1.0 / math.sqrt(2.0))))
    density = jnp.exp(-0.5 * pre_act * pre_act) * (1.0 / math.sqrt(2.0 * math.pi))
    return (pre_act * normal_cdf, normal_cdf + pre_act * density)

def reference(field, spectral_weight, local_weight, cotangent):
    field = field.astype(jnp.float32)
    cotangent = cotangent.astype(jnp.float32)
    chans, total_steps, cells_x, cells_y, cells_z = field.shape
    factor = 1.0 / math.sqrt(total_steps * cells_x * cells_y * cells_z)
    tables = all_tables(total_steps, cells_x, cells_y, cells_z)
    weight_real = spectral_weight[0]
    weight_imag = spectral_weight[1]
    spec_real, spec_imag = analyse(field, tables, factor)
    mixed_real = contract('ckpm,kpmcd->dkpm', spec_real, weight_real) - contract('ckpm,kpmcd->dkpm', spec_imag, weight_imag)
    mixed_imag = contract('ckpm,kpmcd->dkpm', spec_real, weight_imag) + contract('ckpm,kpmcd->dkpm', spec_imag, weight_real)
    pre_act = contract('cd,ctxyz->dtxyz', local_weight, field) + synthesise(mixed_real, mixed_imag, tables, factor)
    layer_out, derivative = gelu_parts(pre_act)
    upstream = cotangent * derivative
    grad_real, grad_imag = analyse(upstream, tables, factor)
    weights = time_weights()[None, None, :, None, None]
    out_real = contract('ckpm,dkpm->kpmcd', spec_real, grad_real) + contract('ckpm,dkpm->kpmcd', spec_imag, grad_imag)
    out_imag = contract('ckpm,dkpm->kpmcd', spec_real, grad_imag) - contract('ckpm,dkpm->kpmcd', spec_imag, grad_real)
    grad_spectral = jnp.stack([out_real * weights, out_imag * weights], 0)
    back_real = contract('dkpm,kpmcd->ckpm', grad_real, weight_real) + contract('dkpm,kpmcd->ckpm', grad_imag, weight_imag)
    back_imag = contract('dkpm,kpmcd->ckpm', grad_imag, weight_real) - contract('dkpm,kpmcd->ckpm', grad_real, weight_imag)
    grad_field = contract('cd,dtxyz->ctxyz', local_weight, upstream) + synthesise(back_real, back_imag, tables, factor)
    return (layer_out, grad_field, grad_spectral)
```

```python
import functools
import math

import jax
import jax.numpy as jnp
import ml_dtypes
import numpy as np
from jax import lax
from jax.experimental import pallas as pl
from jax.experimental.pallas import tpu as pltpu
from jax.sharding import PartitionSpec as P

KT = 4
STRIDE = 32
LANES = 128
F32 = jnp.float32
BF16 = jnp.bfloat16


class Sizes:
    def __init__(self, gx, ta, chans, kf, cells):
        self.gx, self.ta, self.chans, self.kf, self.cells = gx, ta, chans, kf, cells
        self.nxc = 8 if gx % 8 == 0 else 2
        self.ny = gx // self.nxc
        self.pb = kf * kf // gx
        self.ib = kf // ta
        self.width = 2 * chans
        self.per = LANES // self.width
        self.tiles = -(-self.pb // self.per)
        self.rows = 8 * ta
        self.modes = self.ib * self.pb * KT
        self.fper = LANES // STRIDE
        self.ftiles = -(-kf // self.fper)


def split(table):
    table = table.astype(np.float32)
    high = table.astype(ml_dtypes.bfloat16)
    low = (table - high.astype(np.float32)).astype(ml_dtypes.bfloat16)
    return high, low


def two_terms(table):
    high, low = split(table)
    return np.concatenate(
        [np.concatenate([high, high], 1), np.concatenate([low, np.zeros_like(low)], 1)], 0
    )


def make_tables(n):
    half = n.kf // 2
    freq = np.where(np.arange(n.kf) < half, np.arange(n.kf), np.arange(n.kf) - n.kf)
    angle = 2 * np.pi * ((np.arange(n.cells)[:, None] * freq[None, :]) % n.cells) / n.cells
    cos, sin = np.cos(angle), np.sin(angle)
    grid_in = two_terms(np.concatenate([cos.T, sin.T], 0))
    along_z = np.concatenate(
        [np.concatenate([cos.T, sin.T], 1), np.concatenate([-sin.T, cos.T], 1)], 0
    )
    high, low = split(along_z)
    z_out = np.zeros((2 * LANES, 2 * n.cells), ml_dtypes.bfloat16)
    z_out[: 2 * n.kf] = high
    z_out[2 * n.kf : 4 * n.kf] = high
    z_out[LANES : LANES + 2 * n.kf] = low
    high, low = split(np.concatenate([cos, -sin], 1))
    y_out = np.concatenate([high, high, low], 1)
    cells_x = n.gx
    place = np.arange(cells_x)
    sent_by = (place % n.ny) * n.nxc + place // n.ny
    freq_rows = np.zeros((n.rows,), np.int64)
    used = np.zeros((n.rows,), np.float64)
    for block in range(n.ta):
        for i in range(n.ib):
            freq_rows[8 * block + i] = freq[block * n.ib + i]
            used[8 * block + i] = 1.0
    angle = 2 * np.pi * ((freq_rows[:, None] * sent_by[None, :]) % cells_x) / cells_x
    x_in = two_terms(
        np.concatenate([np.cos(angle), -np.sin(angle)], 1) * used[:, None]
    )
    angle = 2 * np.pi * ((place[:, None] * freq_rows[None, :]) % cells_x) / cells_x
    x_out = two_terms(
        np.concatenate([np.cos(angle) * used, np.sin(angle) * used], 1)
    )
    return grid_in, z_out, y_out, x_in, x_out


def halves(value):
    high = value.astype(BF16).astype(F32)
    return high, value - high


def dot(left, right):
    return jnp.dot(left, right, preferred_element_type=F32)


def roll(value, amount):
    amount = amount % LANES
    return value if amount == 0 else pltpu.roll(value, amount, 1)


def times_i(value, chans):
    lane = lax.broadcasted_iota(jnp.int32, value.shape, 1)
    return jnp.where(lane % (2 * chans) < chans, -roll(value, -chans), roll(value, chans))


def kernel(
    n,
    factor,
    field,
    cotangent,
    weight,
    local,
    grid_in,
    z_out,
    y_out,
    x_in,
    x_out,
    layer_out,
    grad_field,
    spec_out,
    grad_out,
    mixed_local,
    upstream,
    y_cos,
    y_sin,
    z_real,
    z_imag,
    pairs,
    stacked,
    turned,
    sent,
    got,
    send_sem,
    recv_sem,
):
    chans, kf, cells = n.chans, n.kf, n.cells
    gx, ta = lax.axis_index("gx"), lax.axis_index("ta")
    my_y, my_xc = gx // n.nxc, gx % n.nxc
    mesh_ids = pl.DeviceIdType.MESH

    def y_peer(k):
        peer = lax.rem(my_y + k, n.ny)
        return peer, {"gx": peer * n.nxc + my_xc, "ta": ta}

    def xc_peer(k):
        peer = lax.rem(my_xc + k, n.nxc)
        return peer, {"gx": my_y * n.nxc + peer, "ta": ta}

    def t_peer(k):
        peer = lax.rem(ta + k, n.ta)
        return peer, {"gx": gx, "ta": peer}

    along = {
        "y": (n.ny, my_y, y_peer, n.nxc),
        "xc": (n.nxc, my_xc, xc_peer, n.ny),
        "t": (n.ta, ta, t_peer, 8),
    }

    barrier = pltpu.get_barrier_semaphore()
    others = 0
    for axis in ("y", "xc", "t"):
        count, _, peer_of, _ = along[axis]
        for k in range(1, count):
            _, device = peer_of(k)
            pl.semaphore_signal(barrier, inc=1, device_id=device, device_id_type=mesh_ids)
            others += 1

    def all_blocks(index, count, rows):
        block = got.at[index, :, pl.ds(0, (count - 1) * rows), :]
        return pltpu.make_async_remote_copy(
            src_ref=block,
            dst_ref=block,
            send_sem=send_sem.at[index],
            recv_sem=recv_sem.at[index],
            device_id={"gx": gx, "ta": ta},
            device_id_type=mesh_ids,
        )

    def exchange(index, axis):
        count, me, peer_of, rows = along[axis]
        mine = pl.ds(pl.multiple_of(me * rows, rows), rows)
        for k in range(1, count):
            peer, device = peer_of(k)
            pltpu.make_async_remote_copy(
                src_ref=sent.at[index, :, pl.ds(pl.multiple_of(peer * rows, rows), rows), :],
                dst_ref=got.at[index, :, mine, :],
                send_sem=send_sem.at[index],
                recv_sem=recv_sem.at[index],
                device_id=device,
                device_id_type=mesh_ids,
            ).start()
        for q in range(n.tiles):
            got[index, q, mine, :] = sent[index, q, mine, :]

    def arrived(index, axis):
        count, _, _, rows = along[axis]
        all_blocks(index, count, rows).wait_recv()

    def regroup(index):
        for q in range(n.tiles):
            for xc in range(n.nxc):
                sent[index + 1, q, xc * n.ny : (xc + 1) * n.ny, :] = got[
                    index, q, pl.ds(xc, n.ny, stride=n.nxc), :
                ]

    def mix_local(source, transposed, start, stop):
        def step(at, carry):
            rows = pl.ds(pl.multiple_of(at * 16, 16), 16)
            values = [source[c, rows, :].astype(F32) for c in range(chans)]
            for d in range(chans):
                total = None
                for c in range(chans):
                    scale = local[d, c] if transposed else local[c, d]
                    term = values[c] * scale
                    total = term if total is None else total + term
                mixed_local[d, rows, :] = total
            return carry

        lax.fori_loop(start, stop, step, 0)

    def pack(index):
        parts = []
        for source in (y_cos, y_sin):
            high, low = halves(source[...])
            both = jnp.concatenate([high.astype(BF16), low.astype(BF16)], 1)
            out = lax.dot_general(
                grid_in[...], both, (((1,), (1,)), ((), ())), preferred_element_type=F32
            )
            parts.append(out[: 2 * kf] + out[2 * kf :])
        of_cos, of_sin = parts
        real = of_cos[:kf] - of_sin[kf:]
        imag = -(of_sin[:kf] + of_cos[kf:])
        lane = lax.broadcasted_iota(jnp.int32, (kf, LANES), 1)
        for j in range(kf):
            tile = slice((j // n.fper) * LANES, (j // n.fper + 1) * LANES)
            back = (j % n.fper) * STRIDE
            value = jnp.where(
                lane < chans,
                roll(real[:, tile], -back),
                jnp.where(lane < 2 * chans, roll(imag[:, tile], chans - back), 0.0),
            )
            pairs[j * kf : (j + 1) * kf, :] = value
        for q in range(n.tiles):
            total = None
            for r in range(n.per):
                value = roll(pairs[pl.ds(q * n.per + r, n.gx, stride=n.pb), :], r * n.width)
                total = value if total is None else total + value
            sent[index, q, : n.gx, :] = total

    def unpack(index):
        for q in range(n.tiles):
            for r in range(n.per):
                value = roll(got[index, q, : n.gx, :], -r * n.width)
                for xc in range(n.nxc):
                    pairs[
                        pl.ds(n.pb * xc + q * n.per + r, n.ny, stride=n.pb * n.nxc), :
                    ] = value[xc * n.ny : (xc + 1) * n.ny]
        lane = lax.broadcasted_iota(jnp.int32, (kf, LANES), 1)
        for tile in range(n.ftiles):
            real = jnp.zeros((kf, LANES), F32)
            imag = jnp.zeros((kf, LANES), F32)
            for part in range(n.fper):
                j = tile * n.fper + part
                if j >= kf:
                    continue
                value = pairs[j * kf : (j + 1) * kf, :]
                begin = part * STRIDE
                here = (lane >= begin) & (lane < begin + chans)
                real = jnp.where(here, roll(value, begin), real)
                imag = jnp.where(here, roll(value, begin - chans), imag)
            high, low = halves(jnp.concatenate([real, imag], 0))
            pad = jnp.zeros((LANES - 4 * kf, LANES), F32)
            rows = jnp.concatenate([high, low, pad], 0).T.astype(BF16)
            out = dot(jnp.concatenate([rows, rows], 1), z_out[...])
            z_real[tile * LANES : (tile + 1) * LANES, :] = out[:, :cells]
            z_imag[tile * LANES : (tile + 1) * LANES, :] = out[:, cells:]

    def plane(d):
        rows = pl.ds(d, kf, stride=STRIDE)
        high, low = halves(jnp.concatenate([z_real[rows, :], z_imag[rows, :]], 0))
        return dot(y_out[...], jnp.concatenate([high, low, high], 0).astype(BF16))

    def put_y(d, out):
        rows = pl.ds(d, kf, stride=STRIDE)
        y_cos[rows, :] = out[:kf] + out[2 * kf : 3 * kf]
        y_sin[rows, :] = out[kf : 2 * kf] + out[3 * kf :]

    def along_x(table, source, target, rows):
        for q in range(n.tiles):
            value = got[source, q, :rows, :]
            high, low = halves(jnp.concatenate([value, times_i(value, chans)], 0))
            out = dot(table[...], jnp.concatenate([high, low], 0).astype(BF16))
            half = out.shape[0] // 2
            sent[target, q, :half, :] = out[:half] + out[half:]

    def time_in(index, target):
        for q in range(n.tiles):
            steps = [got[index, q, 8 * t : 8 * t + 8, :] for t in range(n.ta)]
            for m in range(KT):
                real = imag = None
                for t in range(n.ta):
                    angle = 2 * math.pi * ((m * t) % n.ta) / n.ta
                    first = steps[t] * (math.cos(angle) * factor)
                    second = steps[t] * (math.sin(angle) * factor)
                    real = first if real is None else real + first
                    imag = second if imag is None else imag + second
                value = real - times_i(imag, chans)
                for r in range(n.per):
                    stacked[
                        pl.ds((q * n.per + r) * KT + m, n.ib, stride=n.pb * KT), :
                    ] = roll(value, -r * n.width)[: n.ib]
        target[...] = stacked[...].T[: n.width]

    def time_out(index):
        stacked[...] = turned[...].T
        weights = [1.0 if m == 0 else 2.0 for m in range(KT)]
        for q in range(n.tiles):
            values = []
            for m in range(KT):
                total = None
                for r in range(n.per):
                    rows = pl.ds((q * n.per + r) * KT + m, n.ib, stride=n.pb * KT)
                    value = roll(stacked[rows, :], r * n.width)
                    total = value if total is None else total + value
                values.append((total, times_i(total, chans)))
            for t in range(n.ta):
                total = None
                for m in range(KT):
                    angle = 2 * math.pi * ((m * t) % n.ta) / n.ta
                    value = values[m][0] * (math.cos(angle) * factor * weights[m])
                    value += values[m][1] * (math.sin(angle) * factor * weights[m])
                    total = value if total is None else total + value
                sent[index, q, 8 * t : 8 * t + n.ib, :] = total

    def analyse_field(c, carry):
        put_y(c, dot(grid_in[:, :cells], field[c]))
        return carry

    lax.fori_loop(0, chans, analyse_field, 0)
    pack(0)
    stacked[...] = jnp.zeros_like(stacked)
    turned[...] = jnp.zeros_like(turned)
    for index in (3, 9):
        sent[index] = jnp.zeros_like(sent[index])
    pl.semaphore_wait(barrier, others)

    def to_owner(index, result, hidden):
        exchange(index, "y")
        hidden(0)
        arrived(index, "y")
        regroup(index)
        exchange(index + 1, "xc")
        hidden(1)
        arrived(index + 1, "xc")
        along_x(x_in, index + 1, index + 2, n.gx)
        exchange(index + 2, "t")
        hidden(2)
        arrived(index + 2, "t")
        time_in(index + 2, result)

    def to_planes(index, hidden):
        time_out(index)
        exchange(index, "t")
        hidden(3)
        arrived(index, "t")
        along_x(x_out, index, index + 1, n.rows)
        exchange(index + 1, "y")
        hidden(4)
        arrived(index + 1, "y")
        regroup(index + 1)
        exchange(index + 2, "xc")
        hidden(5)
        arrived(index + 2, "xc")
        unpack(index + 2)

    chunks = cells // 16
    cuts = [0, chunks // 4, chunks // 2, chunks // 2, chunks // 2, 3 * chunks // 4, chunks]

    def hidden_field(part):
        if cuts[part + 1] > cuts[part]:
            mix_local(field, False, cuts[part], cuts[part + 1])

    def hidden_upstream(part):
        if cuts[part + 1] > cuts[part]:
            mix_local(upstream, True, cuts[part], cuts[part + 1])

    to_owner(0, spec_out, hidden_field)
    real = jnp.zeros((chans, LANES), F32)
    imag = jnp.zeros((chans, LANES), F32)
    for c in range(chans):
        spec_r, spec_i = spec_out[c : c + 1, :], spec_out[chans + c : chans + c + 1, :]
        real += spec_r * weight[0, c] - spec_i * weight[1, c]
        imag += spec_r * weight[1, c] + spec_i * weight[0, c]
    turned[:chans, :] = real
    turned[chans : 2 * chans, :] = imag
    to_planes(3, hidden_field)

    def activate(d, carry):
        pre_act = mixed_local[d] + plane(d)
        normal_cdf = 0.5 * (1.0 + lax.erf(pre_act * (1.0 / math.sqrt(2.0))))
        density = jnp.exp(-0.5 * pre_act * pre_act) * (1.0 / math.sqrt(2.0 * math.pi))
        layer_out[d] = pre_act * normal_cdf
        value = cotangent[d].astype(F32) * (normal_cdf + pre_act * density)
        upstream[d] = value
        high, low = halves(value)
        both = jnp.concatenate([high, low], 0).astype(BF16)
        put_y(d, dot(grid_in[...], both))
        return carry

    lax.fori_loop(0, chans, activate, 0)
    pack(6)
    to_owner(6, grad_out, hidden_upstream)
    grad_r, grad_i = grad_out[:chans, :], grad_out[chans : 2 * chans, :]
    for c in range(chans):
        turned[c : c + 1, :] = jnp.sum(
            weight[0, c] * grad_r + weight[1, c] * grad_i, 0, keepdims=True
        )
        turned[chans + c : chans + c + 1, :] = jnp.sum(
            weight[0, c] * grad_i - weight[1, c] * grad_r, 0, keepdims=True
        )
    to_planes(9, hidden_upstream)

    def finish(c, carry):
        grad_field[c] = mixed_local[c] + plane(c)
        return carry

    lax.fori_loop(0, chans, finish, 0)
    for index, axis in enumerate(("y", "xc", "t", "t", "y", "xc") * 2):
        count, _, _, rows = along[axis]
        all_blocks(index, count, rows).wait_send()


def shards(n, factor, field, spectral_weight, local_weight, cotangent):
    chans, cells = n.chans, n.cells
    tables = [jnp.asarray(table) for table in make_tables(n)]
    weight = spectral_weight.reshape(2, n.modes, chans, chans)
    weight = jnp.transpose(weight, (0, 2, 3, 1))
    weight = jnp.pad(weight, ((0, 0), (0, 0), (0, 0), (0, LANES - n.modes)))
    whole = pl.BlockSpec(memory_space=pltpu.VMEM)
    wide = jax.ShapeDtypeStruct((chans, cells, cells), F32)
    small = jax.ShapeDtypeStruct((n.width, LANES), F32)
    layer_out, grad_field, spec, grad = pl.pallas_call(
        functools.partial(kernel, n, factor),
        out_shape=(wide, wide, small, small),
        in_specs=[whole] * 3 + [pl.BlockSpec(memory_space=pltpu.SMEM)] + [whole] * 5,
        out_specs=(whole,) * 4,
        scratch_shapes=[
            pltpu.VMEM((chans, cells, cells), F32),
            pltpu.VMEM((chans, cells, cells), F32),
            pltpu.VMEM((n.ftiles * LANES, cells), F32),
            pltpu.VMEM((n.ftiles * LANES, cells), F32),
            pltpu.VMEM((n.ftiles * LANES, cells), F32),
            pltpu.VMEM((n.ftiles * LANES, cells), F32),
            pltpu.VMEM((n.kf * n.kf, LANES), F32),
            pltpu.VMEM((LANES, LANES), F32),
            pltpu.VMEM((LANES, LANES), F32),
            pltpu.VMEM((12, n.tiles, max(n.gx, n.rows), LANES), F32),
            pltpu.VMEM((12, n.tiles, max(n.gx, n.rows), LANES), F32),
            pltpu.SemaphoreType.DMA((12,)),
            pltpu.SemaphoreType.DMA((12,)),
        ],
        compiler_params=pltpu.CompilerParams(
            collective_id=0, has_side_effects=True, vmem_limit_bytes=48 * 1024 * 1024
        ),
    )(
        field.reshape(chans, cells, cells),
        cotangent.reshape(chans, cells, cells),
        weight,
        local_weight,
        *tables,
    )
    pairs_shape = (n.ib, n.pb, KT, chans)
    spec_r = spec[:chans, : n.modes].T.reshape(pairs_shape)[..., :, None]
    spec_i = spec[chans:, : n.modes].T.reshape(pairs_shape)[..., :, None]
    grad_r = grad[:chans, : n.modes].T.reshape(pairs_shape)[..., None, :]
    grad_i = grad[chans:, : n.modes].T.reshape(pairs_shape)[..., None, :]
    weights = jnp.where(jnp.arange(KT) == 0, 1.0, 2.0).astype(F32)[None, None, :, None, None]
    spec_r, spec_i = spec_r * weights, spec_i * weights
    grad_spectral = jnp.stack(
        [spec_r * grad_r + spec_i * grad_i, spec_r * grad_i - spec_i * grad_r], 0
    )
    return (layer_out.reshape(field.shape), grad_field.reshape(field.shape), grad_spectral)


def solution(mesh, chans=20, kf=24, cells=128):
    n = Sizes(mesh.shape["gx"], mesh.shape["ta"], chans, kf, cells)
    factor = 1.0 / math.sqrt(n.gx * n.ta * cells * cells)
    grid = P(None, "ta", "gx", None, None)
    modes = P(None, "ta", "gx", None, None, None)
    return jax.shard_map(
        functools.partial(shards, n, factor),
        mesh=mesh,
        in_specs=(grid, modes, P(), grid),
        out_specs=(grid, grid, modes),
        check_vma=False,
    )
```

```python
import functools
import math

import jax
import jax.numpy as jnp
import ml_dtypes
import numpy as np
from jax import lax
from jax.experimental import pallas as pl
from jax.experimental.pallas import tpu as pltpu
from jax.sharding import PartitionSpec as P

KT = 4
STRIDE = 32
LANES = 128
F32 = jnp.float32
BF16 = jnp.bfloat16


class Sizes:
    def __init__(self, gx, ta, chans, kf, cells):
        self.gx, self.ta, self.chans, self.kf, self.cells = gx, ta, chans, kf, cells
        self.nx = 4 if gx % 8 == 0 else 1
        self.ny = gx // (2 * self.nx)
        self.pb = kf * kf // gx
        self.ib = kf // ta
        self.width = 2 * chans
        self.per = LANES // self.width
        self.tiles = -(-self.pb // self.per)
        self.rows = 4 * ta
        self.blocks = self.ib * self.pb
        self.modes = self.blocks * KT
        self.fper = LANES // STRIDE
        self.ftiles = -(-kf // self.fper)
        self.frows = self.ftiles * LANES


def split(table):
    table = table.astype(np.float32)
    high = table.astype(ml_dtypes.bfloat16)
    low = (table - high.astype(np.float32)).astype(ml_dtypes.bfloat16)
    return high, low


def two_terms(table):
    high, low = split(table)
    return np.concatenate(
        [np.concatenate([high, high], 1), np.concatenate([low, np.zeros_like(low)], 1)], 0
    )


def make_tables(n):
    half = n.kf // 2
    freq = np.where(np.arange(n.kf) < half, np.arange(n.kf), np.arange(n.kf) - n.kf)
    angle = 2 * np.pi * ((np.arange(n.cells)[:, None] * freq[None, :]) % n.cells) / n.cells
    cos, sin = np.cos(angle), np.sin(angle)
    grid_in = two_terms(np.concatenate([cos.T, sin.T], 0))
    along_z = np.concatenate(
        [np.concatenate([cos.T, sin.T], 1), np.concatenate([-sin.T, cos.T], 1)], 0
    )
    high, low = split(along_z)
    z_out = np.zeros((2 * LANES, 2 * n.cells), ml_dtypes.bfloat16)
    z_out[: 2 * n.kf] = high
    z_out[2 * n.kf : 4 * n.kf] = high
    z_out[LANES : LANES + 2 * n.kf] = low
    high, low = split(np.concatenate([cos, -sin], 1))
    y_out = np.concatenate([high, high, low], 1)
    place = np.arange(n.gx)
    freq_rows = np.zeros((n.rows,), np.int64)
    used = np.zeros((n.rows,), np.float64)
    for block in range(n.ta):
        for i in range(n.ib):
            freq_rows[4 * block + i] = freq[block * n.ib + i]
            used[4 * block + i] = 1.0
    angle = 2 * np.pi * ((freq_rows[:, None] * place[None, :]) % n.gx) / n.gx
    x_in = two_terms(np.concatenate([np.cos(angle), -np.sin(angle)], 1) * used[:, None])
    angle = angle.T
    x_out = two_terms(np.concatenate([np.cos(angle) * used, np.sin(angle) * used], 1))
    places, parts, begin = {}, [], 0
    for name, part in (
        ("grid_in", grid_in),
        ("z_out", z_out),
        ("y_out", y_out),
        ("x_in", x_in),
        ("x_out", x_out),
    ):
        rows = -(-part.shape[0] // 16) * 16
        padded = np.zeros((rows, 256), ml_dtypes.bfloat16)
        padded[: part.shape[0], : part.shape[1]] = part
        places[name] = (slice(begin, begin + part.shape[0]), slice(0, part.shape[1]))
        parts.append(padded)
        begin += rows
    return np.concatenate(parts, 0), places


def halves(value):
    high = value.astype(BF16).astype(F32)
    return high, value - high


def dot(left, right):
    return jnp.dot(left, right, preferred_element_type=F32)


def roll(value, amount):
    amount = amount % LANES
    return value if amount == 0 else pltpu.roll(value, amount, 1)


def times_i(value, chans):
    lane = lax.broadcasted_iota(jnp.int32, value.shape, 1)
    return jnp.where(lane % (2 * chans) < chans, -roll(value, -chans), roll(value, chans))


def far_first(step, count):
    return count // 2 + (1 - 2 * (step % 2)) * ((step + 1) // 2)


def synthesis(n, y_out, z_real, z_imag, first):
    sides = []
    for d in (first, first + 1):
        rows = pl.ds(d, n.kf, stride=STRIDE)
        sides.append(jnp.concatenate([z_real[rows, :], z_imag[rows, :]], 0))
    high, low = halves(jnp.concatenate(sides, 1))
    return dot(y_out[...], jnp.concatenate([high, low, high], 0).astype(BF16))


def side_by_side(ref, first):
    return jnp.concatenate([ref[first], ref[first + 1]], 1)


def kernel(
    n,
    factor,
    places,
    field_hbm,
    cotangent_hbm,
    weight_hbm,
    local_hbm,
    tables_hbm,
    layer_out,
    mixed_local,
    z_real,
    z_imag,
    grad_out,
    field,
    cotangent,
    weight_in,
    local,
    tables,
    weight,
    upstream,
    y_cos,
    y_sin,
    pairs,
    stacked,
    turned,
    spec,
    spec_rows,
    grad_rows,
    sent_x,
    got_x,
    sent_t,
    got_t,
    load_sem,
    own_sem,
    send_sem,
    recv_sem,
):
    chans, kf, cells = n.chans, n.kf, n.cells
    gx, ta = lax.axis_index("gx"), lax.axis_index("ta")
    my_y, my_x, my_core = gx // (2 * n.nx), (gx // 2) % n.nx, gx % 2
    mesh_ids = pl.DeviceIdType.MESH
    grid_in, z_out, y_out, x_in, x_out = (
        tables.at[places[name]] for name in ("grid_in", "z_out", "y_out", "x_in", "x_out")
    )

    def x_peer(step):
        y = lax.rem(my_y + far_first(step // (2 * n.nx), n.ny), n.ny)
        x = lax.rem(my_x + far_first((step // 2) % n.nx, n.nx), n.nx)
        core = lax.rem(my_core + 1 - step % 2, 2)
        return (y * n.nx + x) * 2 + core

    def t_peer(step):
        return lax.rem(ta + far_first(step, n.ta), n.ta)

    barrier = pltpu.get_barrier_semaphore()

    def greet_x(step, carry):
        pl.semaphore_signal(
            barrier, inc=1, device_id={"gx": x_peer(step), "ta": ta}, device_id_type=mesh_ids
        )
        return carry

    for step in range(n.ta - 1):
        pl.semaphore_signal(
            barrier, inc=1, device_id={"gx": gx, "ta": t_peer(step)}, device_id_type=mesh_ids
        )
    loads = [
        pltpu.make_async_copy(source, target, load_sem.at[at])
        for at, (source, target) in enumerate(
            (
                (tables_hbm, tables),
                (field_hbm, field),
                (local_hbm, local),
                (weight_hbm, weight_in),
                (cotangent_hbm, cotangent),
            )
        )
    ]
    for load in loads:
        load.start()
    lax.fori_loop(0, n.gx - 1, greet_x, 0)

    def received(block, index):
        return pltpu.make_async_remote_copy(
            src_ref=block,
            dst_ref=block,
            send_sem=send_sem.at[index],
            recv_sem=recv_sem.at[index],
            device_id={"gx": gx, "ta": ta},
            device_id_type=mesh_ids,
        )

    def all_x(index):
        return received(got_x.at[index // 2, pl.ds(0, (n.gx - 1) * n.tiles), :], index)

    def all_t(index):
        return received(got_t.at[index // 2, :, pl.ds(0, (n.ta - 1) * 4), :], index)

    def of_x(ref, index, device):
        return ref.at[index // 2, pl.ds(pl.multiple_of(4 * device, 4), n.tiles), :]

    def of_t(ref, index, device):
        return ref.at[index // 2, :, pl.ds(pl.multiple_of(4 * device, 4), 4), :]

    def exchange_x(index):
        def send(step, carry):
            peer = x_peer(step)
            pltpu.make_async_remote_copy(
                src_ref=of_x(sent_x, index, peer),
                dst_ref=of_x(got_x, index, gx),
                send_sem=send_sem.at[index],
                recv_sem=recv_sem.at[index],
                device_id={"gx": peer, "ta": ta},
                device_id_type=mesh_ids,
            ).start()
            return carry

        lax.fori_loop(0, n.gx - 1, send, 0, unroll=7 if (n.gx - 1) % 7 == 0 else 1)
        pltpu.make_async_copy(
            of_x(sent_x, index, gx), of_x(got_x, index, gx), own_sem.at[index]
        ).start()

    def exchange_t(index):
        for step in range(n.ta - 1):
            peer = t_peer(step)
            pltpu.make_async_remote_copy(
                src_ref=of_t(sent_t, index, peer),
                dst_ref=of_t(got_t, index, ta),
                send_sem=send_sem.at[index],
                recv_sem=recv_sem.at[index],
                device_id={"gx": gx, "ta": peer},
                device_id_type=mesh_ids,
            ).start()
        pltpu.make_async_copy(
            of_t(sent_t, index, ta), of_t(got_t, index, ta), own_sem.at[index]
        ).start()

    def arrived_x(index):
        pltpu.make_async_copy(
            of_x(sent_x, index, gx), of_x(got_x, index, gx), own_sem.at[index]
        ).wait()
        all_x(index).wait_recv()

    def arrived_t(index):
        pltpu.make_async_copy(
            of_t(sent_t, index, ta), of_t(got_t, index, ta), own_sem.at[index]
        ).wait()
        all_t(index).wait_recv()

    def mix_local(source, transposed, start, stop):
        def step(at, carry):
            rows = pl.ds(pl.multiple_of(at * 16, 16), 16)
            values = [source[c, rows, :].astype(F32) for c in range(chans)]
            for d in range(chans):
                total = None
                for c in range(chans):
                    scale = local[d, c] if transposed else local[c, d]
                    term = values[c] * scale
                    total = term if total is None else total + term
                mixed_local[d, rows, :] = total
            return carry

        lax.fori_loop(start, stop, step, 0)

    def turn_weights(part):
        def step(c, carry):
            for block in range(n.blocks):
                pairs[KT * block : KT * block + KT, :chans] = weight_in[part * n.blocks + block, c]
            weight[part, c] = pairs[:LANES, :].T[:chans]
            return carry

        pairs[:LANES, :] = jnp.zeros((LANES, LANES), F32)
        lax.fori_loop(0, chans, step, 0)

    def pack(index):
        parts = []
        for source in (y_cos, y_sin):
            high, low = halves(source[...])
            both = jnp.concatenate([high.astype(BF16), low.astype(BF16)], 1)
            out = lax.dot_general(
                grid_in[...], both, (((1,), (1,)), ((), ())), preferred_element_type=F32
            )
            parts.append(out[: 2 * kf] + out[2 * kf :])
        of_cos, of_sin = parts
        real = of_cos[:kf] - of_sin[kf:]
        imag = -(of_sin[:kf] + of_cos[kf:])
        lane = lax.broadcasted_iota(jnp.int32, (kf, LANES), 1)
        for j in range(kf):
            tile = slice((j // n.fper) * LANES, (j // n.fper + 1) * LANES)
            back = (j % n.fper) * STRIDE
            value = jnp.where(
                lane < chans,
                roll(real[:, tile], -back),
                jnp.where(lane < 2 * chans, roll(imag[:, tile], chans - back), 0.0),
            )
            pairs[j * kf : (j + 1) * kf, :] = value
        for q in range(n.tiles):
            total = None
            for r in range(n.per):
                value = roll(pairs[pl.ds(q * n.per + r, n.gx, stride=n.pb), :], r * n.width)
                total = value if total is None else total + value
            sent_x[index // 2, pl.ds(q, n.gx, stride=4), :] = total

    def unpack(index):
        for q in range(n.tiles):
            received_rows = got_x[index // 2, pl.ds(q, n.gx, stride=4), :]
            for r in range(n.per):
                pairs[pl.ds(q * n.per + r, n.gx, stride=n.pb), :] = roll(
                    received_rows, -r * n.width
                )
        lane = lax.broadcasted_iota(jnp.int32, (kf, LANES), 1)
        for tile in range(n.ftiles):
            real = jnp.zeros((kf, LANES), F32)
            imag = jnp.zeros((kf, LANES), F32)
            for part in range(n.fper):
                j = tile * n.fper + part
                if j >= kf:
                    continue
                value = pairs[j * kf : (j + 1) * kf, :]
                begin = part * STRIDE
                here = (lane >= begin) & (lane < begin + chans)
                real = jnp.where(here, roll(value, begin), real)
                imag = jnp.where(here, roll(value, begin - chans), imag)
            high, low = halves(jnp.concatenate([real, imag], 0))
            pad = jnp.zeros((LANES - 4 * kf, LANES), F32)
            rows = jnp.concatenate([high, low, pad], 0).T.astype(BF16)
            out = dot(jnp.concatenate([rows, rows], 1), z_out[...])
            z_real[tile * LANES : (tile + 1) * LANES, :] = out[:, :cells]
            z_imag[tile * LANES : (tile + 1) * LANES, :] = out[:, cells:]

    def put_y(first, out):
        out = out[: 2 * kf] + out[2 * kf :]
        for side in range(2):
            rows = pl.ds(first + side, kf, stride=STRIDE)
            columns = slice(side * cells, (side + 1) * cells)
            y_cos[rows, :] = out[:kf, columns]
            y_sin[rows, :] = out[kf:, columns]

    def along_x(table, value):
        high, low = halves(jnp.concatenate([value, times_i(value, chans)], 0))
        out = dot(table[...], jnp.concatenate([high, low], 0).astype(BF16))
        half = out.shape[0] // 2
        return out[:half] + out[half:]

    def analysis_x(index):
        for q in range(n.tiles):
            value = got_x[index // 2, pl.ds(q, n.gx, stride=4), :]
            sent_t[(index + 1) // 2, q, :, :] = along_x(x_in, value)

    def synthesis_x(index):
        for q in range(n.tiles):
            value = got_t[index // 2, q, :, :]
            sent_x[(index + 1) // 2, pl.ds(q, n.gx, stride=4), :] = along_x(x_out, value)

    upper = lax.broadcasted_iota(jnp.int32, (8, LANES), 0) < 4

    def time_table(kind, m, pair, weight_m):
        first, second = (
            kind(2 * math.pi * ((m * t) % n.ta) / n.ta) * factor * weight_m
            for t in (2 * pair, 2 * pair + 1)
        )
        return first if first == second else jnp.where(upper, first, second)

    def time_in(index):
        for q in range(n.tiles):
            steps = [got_t[index // 2, q, 8 * u : 8 * u + 8, :] for u in range(n.ta // 2)]
            for m in range(KT):
                real = imag = None
                for u in range(n.ta // 2):
                    first = steps[u] * time_table(math.cos, m, u, 1.0)
                    second = steps[u] * time_table(math.sin, m, u, 1.0)
                    real = first if real is None else real + first
                    imag = second if imag is None else imag + second
                value = real - times_i(imag, chans)
                value = value[:4] + value[4:]
                for r in range(n.per):
                    stacked[
                        pl.ds((q * n.per + r) * KT + m, 4, stride=n.pb * KT), :
                    ] = roll(value, -r * n.width)

    def time_out(index):
        stacked[:LANES, :] = turned[...].T
        for q in range(n.tiles):
            values = []
            for m in range(KT):
                total = None
                for r in range(n.per):
                    rows = pl.ds((q * n.per + r) * KT + m, 4, stride=n.pb * KT)
                    value = roll(stacked[rows, :], r * n.width)
                    total = value if total is None else total + value
                total = jnp.concatenate([total, total], 0)
                values.append((total, times_i(total, chans)))
            for u in range(n.ta // 2):
                total = None
                for m in range(KT):
                    scale = 1.0 if m == 0 else 2.0
                    value = values[m][0] * time_table(math.cos, m, u, scale)
                    value += values[m][1] * time_table(math.sin, m, u, scale)
                    total = value if total is None else total + value
                sent_t[index // 2, q, 8 * u : 8 * u + 8, :] = total

    def grad_weights():
        row = lax.broadcasted_iota(jnp.int32, (8, LANES), 0)
        weights = jnp.where(row % KT == 0, 1.0, 2.0)
        for at in range(0, n.modes, 8):
            rows = slice(at, at + 8)
            ours = spec_rows[rows, :] * weights
            real = grad_rows[rows, :]
            imag = roll(real, -chans)
            real, imag = real[:, :chans], imag[:, :chans]
            for c in range(chans):
                spec_r = jnp.broadcast_to(ours[:, c : c + 1], (8, chans))
                spec_i = jnp.broadcast_to(ours[:, chans + c : chans + c + 1], (8, chans))
                out_r = spec_r * real + spec_i * imag
                out_i = spec_r * imag - spec_i * real
                for part in range(2):
                    block = at // KT + part
                    if block < n.blocks:
                        cut = slice(KT * part, KT * part + KT)
                        grad_out[block, c] = out_r[cut]
                        grad_out[n.blocks + block, c] = out_i[cut]

    def analyse_field(pair, carry):
        put_y(2 * pair, dot(grid_in[:, :cells], side_by_side(field, 2 * pair)))
        return carry

    loads[0].wait()
    loads[1].wait()
    lax.fori_loop(0, chans // 2, analyse_field, 0, unroll=2)
    pack(0)
    pl.semaphore_wait(barrier, n.gx - 1 + n.ta - 1)
    exchange_x(0)
    stacked[...] = jnp.zeros_like(stacked)
    turned[...] = jnp.zeros_like(turned)
    loads[3].wait()
    turn_weights(0)
    turn_weights(1)
    loads[2].wait()
    arrived_x(0)
    analysis_x(0)
    exchange_t(1)
    chunks = cells // 16
    mix_local(field, False, 0, 3 * chunks // 8)
    arrived_t(1)
    time_in(1)
    spec[...] = stacked[:LANES, :].T[: n.width]
    real = jnp.zeros((chans, LANES), F32)
    imag = jnp.zeros((chans, LANES), F32)
    for c in range(chans):
        spec_r, spec_i = spec[c : c + 1, :], spec[chans + c : chans + c + 1, :]
        real += spec_r * weight[0, c] - spec_i * weight[1, c]
        imag += spec_r * weight[1, c] + spec_i * weight[0, c]
    turned[:chans, :] = real
    turned[chans : 2 * chans, :] = imag
    spec_rows[...] = stacked[:LANES, :]
    time_out(2)
    exchange_t(2)
    mix_local(field, False, 3 * chunks // 8, 5 * chunks // 8)
    arrived_t(2)
    synthesis_x(2)
    exchange_x(3)
    mix_local(field, False, 5 * chunks // 8, chunks)
    loads[4].wait()
    arrived_x(3)
    unpack(3)

    def activate(pair, carry):
        first = 2 * pair
        pre_act = side_by_side(mixed_local, first) + synthesis(n, y_out, z_real, z_imag, first)
        normal_cdf = 0.5 * (1.0 + lax.erf(pre_act * (1.0 / math.sqrt(2.0))))
        density = jnp.exp(-0.5 * pre_act * pre_act) * (1.0 / math.sqrt(2.0 * math.pi))
        out = pre_act * normal_cdf
        value = side_by_side(cotangent, first).astype(F32) * (normal_cdf + pre_act * density)
        for side in range(2):
            columns = slice(side * cells, (side + 1) * cells)
            layer_out[first + side] = out[:, columns]
            upstream[first + side] = value[:, columns]
        high, low = halves(value)
        put_y(first, dot(grid_in[...], jnp.concatenate([high, low], 0).astype(BF16)))
        return carry

    lax.fori_loop(0, chans // 2, activate, 0, unroll=2)
    pack(4)
    exchange_x(4)
    mix_local(upstream, True, 0, chunks // 2)
    arrived_x(4)
    analysis_x(4)
    exchange_t(5)
    mix_local(upstream, True, chunks // 2, 3 * chunks // 4)
    arrived_t(5)
    time_in(5)
    grad_rows[...] = stacked[:LANES, :]
    spec[...] = stacked[:LANES, :].T[: n.width]
    grad_r, grad_i = spec[:chans, :], spec[chans : 2 * chans, :]
    for c in range(chans):
        turned[c : c + 1, :] = jnp.sum(
            weight[0, c] * grad_r + weight[1, c] * grad_i, 0, keepdims=True
        )
        turned[chans + c : chans + c + 1, :] = jnp.sum(
            weight[0, c] * grad_i - weight[1, c] * grad_r, 0, keepdims=True
        )
    time_out(6)
    exchange_t(6)
    mix_local(upstream, True, 3 * chunks // 4, chunks)
    arrived_t(6)
    synthesis_x(6)
    exchange_x(7)
    grad_weights()
    arrived_x(7)
    unpack(7)
    for index in range(8):
        (all_x if index in (0, 3, 4, 7) else all_t)(index).wait_send()


def finish(
    n,
    layer_in,
    mixed_local,
    z_real,
    z_imag,
    grad_in,
    y_out,
    layer_out,
    grad_field,
    grad_spectral,
    planes,
    sems,
):
    layer_copy = pltpu.make_async_copy(layer_in, layer_out, sems.at[0])
    layer_copy.start()
    grad_copy = pltpu.make_async_copy(grad_in, grad_spectral, sems.at[1])
    grad_copy.start()

    def step(pair, carry):
        first = 2 * pair
        value = side_by_side(mixed_local, first) + synthesis(n, y_out, z_real, z_imag, first)
        for side in range(2):
            planes[first + side] = value[:, side * n.cells : (side + 1) * n.cells]
        two = pl.ds(first, 2)
        pltpu.make_async_copy(planes.at[two], grad_field.at[two], sems.at[2]).start()
        return carry

    lax.fori_loop(0, n.chans // 2, step, 0, unroll=2)
    layer_copy.wait()
    grad_copy.wait()
    pltpu.make_async_copy(planes, grad_field, sems.at[2]).wait()


def shards(n, factor, field, spectral_weight, local_weight, cotangent):
    chans, cells = n.chans, n.cells
    tables, places = make_tables(n)
    weight = jnp.transpose(spectral_weight, (0, 1, 2, 4, 3, 5))
    weight = weight.reshape(2 * n.blocks, chans, KT, chans)
    vmem = pl.BlockSpec(memory_space=pltpu.VMEM)
    hbm = pl.BlockSpec(memory_space=pltpu.HBM)
    wide = jax.ShapeDtypeStruct((chans, cells, cells), F32)
    halfway = jax.ShapeDtypeStruct((n.frows, cells), F32)
    weights = jax.ShapeDtypeStruct(weight.shape, F32)
    rows = max(n.kf * n.kf, LANES)
    results = pl.pallas_call(
        functools.partial(kernel, n, factor, places),
        out_shape=(wide, wide, halfway, halfway, weights),
        in_specs=[hbm] * 5,
        out_specs=(vmem,) * 5,
        scratch_shapes=[
            pltpu.VMEM((chans, cells, cells), BF16),
            pltpu.VMEM((chans, cells, cells), BF16),
            pltpu.VMEM(weight.shape, F32),
            pltpu.SMEM((chans, chans), F32),
            pltpu.VMEM(tables.shape, BF16),
            pltpu.VMEM((2, chans, chans, LANES), F32),
            pltpu.VMEM((chans, cells, cells), F32),
            pltpu.VMEM((n.frows, cells), F32),
            pltpu.VMEM((n.frows, cells), F32),
            pltpu.VMEM((rows, LANES), F32),
            pltpu.VMEM((4 * n.pb * KT, LANES), F32),
            pltpu.VMEM((LANES, LANES), F32),
            pltpu.VMEM((n.width, LANES), F32),
            pltpu.VMEM((LANES, LANES), F32),
            pltpu.VMEM((LANES, LANES), F32),
            pltpu.VMEM((4, 4 * n.gx, LANES), F32),
            pltpu.VMEM((4, 4 * n.gx, LANES), F32),
            pltpu.VMEM((4, n.tiles, n.rows, LANES), F32),
            pltpu.VMEM((4, n.tiles, n.rows, LANES), F32),
            pltpu.SemaphoreType.DMA((5,)),
            pltpu.SemaphoreType.DMA((8,)),
            pltpu.SemaphoreType.DMA((8,)),
            pltpu.SemaphoreType.DMA((8,)),
        ],
        compiler_params=pltpu.CompilerParams(
            collective_id=0, has_side_effects=True, vmem_limit_bytes=40 * 1024 * 1024
        ),
    )(
        *(
            pltpu.with_memory_space_constraint(value, pltpu.HBM)
            for value in (
                field.reshape(chans, cells, cells),
                cotangent.reshape(chans, cells, cells),
                weight,
                local_weight,
                jnp.asarray(tables),
            )
        )
    )
    layer_out, grad_field, grad_spectral = pl.pallas_call(
        functools.partial(finish, n),
        out_shape=(wide, wide, weights),
        in_specs=[vmem] * 6,
        out_specs=(hbm,) * 3,
        scratch_shapes=[
            pltpu.VMEM((chans, cells, cells), F32),
            pltpu.SemaphoreType.DMA((3,)),
        ],
        compiler_params=pltpu.CompilerParams(vmem_limit_bytes=16 * 1024 * 1024),
    )(*results, jnp.asarray(tables[places["y_out"]]))
    grad_spectral = grad_spectral.reshape(2, n.ib, n.pb, chans, KT, chans)
    grad_spectral = jnp.transpose(grad_spectral, (0, 1, 2, 4, 3, 5))
    return (layer_out.reshape(field.shape), grad_field.reshape(field.shape), grad_spectral)


def solution(mesh, chans=20, kf=24, cells=128):
    n = Sizes(mesh.shape["gx"], mesh.shape["ta"], chans, kf, cells)
    factor = 1.0 / math.sqrt(n.gx * n.ta * cells * cells)
    grid = P(None, "ta", "gx", None, None)
    modes = P(None, "ta", "gx", None, None, None)
    return jax.shard_map(
        functools.partial(shards, n, factor),
        mesh=mesh,
        in_specs=(grid, modes, P(), grid),
        out_specs=(grid, grid, modes),
        check_vma=False,
    )
```

```python
import functools
import math

import jax
import jax.numpy as jnp
import ml_dtypes
import numpy as np
from jax import lax
from jax.experimental import pallas as pl
from jax.experimental.pallas import tpu as pltpu
from jax.sharding import PartitionSpec as P

KT = 4
STRIDE = 32
LANES = 128
PIECES = 4
F32 = jnp.float32
BF16 = jnp.bfloat16


class Sizes:
    def __init__(self, gx, ta, chans, kf, cells):
        self.gx, self.ta, self.chans, self.kf, self.cells = gx, ta, chans, kf, cells
        self.nx = 4 if gx % 8 == 0 else 1
        self.ny = gx // (2 * self.nx)
        self.pb = kf * kf // gx
        self.ib = kf // ta
        self.width = 2 * chans
        self.per = LANES // self.width
        self.tiles = -(-self.pb // self.per)
        self.rows = 4 * ta
        self.blocks = self.ib * self.pb
        self.modes = self.blocks * KT
        self.fper = LANES // STRIDE
        self.ftiles = -(-kf // self.fper)
        self.frows = self.ftiles * LANES


def split(table):
    table = table.astype(np.float32)
    high = table.astype(ml_dtypes.bfloat16)
    low = (table - high.astype(np.float32)).astype(ml_dtypes.bfloat16)
    return high, low


def two_terms(table):
    high, low = split(table)
    return np.concatenate(
        [np.concatenate([high, high], 1), np.concatenate([low, np.zeros_like(low)], 1)], 0
    )


def make_tables(n):
    half = n.kf // 2
    freq = np.where(np.arange(n.kf) < half, np.arange(n.kf), np.arange(n.kf) - n.kf)
    angle = 2 * np.pi * ((np.arange(n.cells)[:, None] * freq[None, :]) % n.cells) / n.cells
    cos, sin = np.cos(angle), np.sin(angle)
    grid_in = two_terms(np.concatenate([cos.T, sin.T], 0))
    along_z = np.concatenate(
        [np.concatenate([cos.T, sin.T], 1), np.concatenate([-sin.T, cos.T], 1)], 0
    )
    high, low = split(along_z)
    z_out = np.zeros((2 * LANES, 2 * n.cells), ml_dtypes.bfloat16)
    z_out[: 2 * n.kf] = high
    z_out[2 * n.kf : 4 * n.kf] = high
    z_out[LANES : LANES + 2 * n.kf] = low
    high, low = split(np.concatenate([cos, -sin], 1))
    y_out = np.concatenate([high, high, low], 1)
    place = np.arange(n.gx)
    freq_rows = np.zeros((n.rows,), np.int64)
    used = np.zeros((n.rows,), np.float64)
    for block in range(n.ta):
        for i in range(n.ib):
            freq_rows[4 * block + i] = freq[block * n.ib + i]
            used[4 * block + i] = 1.0
    angle = 2 * np.pi * ((freq_rows[:, None] * place[None, :]) % n.gx) / n.gx
    x_in = two_terms(np.concatenate([np.cos(angle), -np.sin(angle)], 1) * used[:, None])
    angle = angle.T
    x_out = two_terms(np.concatenate([np.cos(angle) * used, np.sin(angle) * used], 1))
    places, parts, begin = {}, [], 0
    for name, part in (
        ("grid_in", grid_in),
        ("z_out", z_out),
        ("y_out", y_out),
        ("x_in", x_in),
        ("x_out", x_out),
    ):
        rows = -(-part.shape[0] // 16) * 16
        padded = np.zeros((rows, 256), ml_dtypes.bfloat16)
        padded[: part.shape[0], : part.shape[1]] = part
        places[name] = (slice(begin, begin + part.shape[0]), slice(0, part.shape[1]))
        parts.append(padded)
        begin += rows
    return np.concatenate(parts, 0), places


def halves(value):
    high = value.astype(BF16).astype(F32)
    return high, value - high


def dot(left, right):
    return jnp.dot(left, right, preferred_element_type=F32)


def roll(value, amount):
    amount = amount % LANES
    return value if amount == 0 else pltpu.roll(value, amount, 1)


def times_i(value, chans):
    lane = lax.broadcasted_iota(jnp.int32, value.shape, 1)
    return jnp.where(lane % (2 * chans) < chans, -roll(value, -chans), roll(value, chans))


def far_first(step, count):
    return count // 2 + (1 - 2 * (step % 2)) * ((step + 1) // 2)


def synthesis(n, y_out, z_real, z_imag, first):
    sides = []
    for d in (first, first + 1):
        rows = pl.ds(d, n.kf, stride=STRIDE)
        sides.append(jnp.concatenate([z_real[rows, :], z_imag[rows, :]], 0))
    high, low = halves(jnp.concatenate(sides, 1))
    return dot(y_out[...], jnp.concatenate([high, low, high], 0).astype(BF16))


def side_by_side(ref, first):
    return jnp.concatenate([ref[first], ref[first + 1]], 1)


def kernel(
    n,
    factor,
    places,
    field_hbm,
    cotangent_hbm,
    weight_hbm,
    local_hbm,
    tables_hbm,
    layer_out,
    mixed_local,
    z_real,
    z_imag,
    grad_out,
    field,
    cotangent,
    weight_in,
    local,
    tables,
    weight,
    upstream,
    y_cos,
    y_sin,
    pairs,
    stacked,
    turned,
    spec,
    spec_rows,
    grad_rows,
    sent_x,
    got_x,
    sent_t,
    got_t,
    load_sem,
    own_sem,
    send_sem,
    recv_sem,
):
    chans, kf, cells = n.chans, n.kf, n.cells
    gx, ta = lax.axis_index("gx"), lax.axis_index("ta")
    my_y, my_x, my_core = lax.div(gx, 2 * n.nx), lax.rem(lax.div(gx, 2), n.nx), lax.rem(gx, 2)
    mesh_ids = pl.DeviceIdType.MESH
    grid_in, z_out, y_out, x_in, x_out = (
        tables.at[places[name]] for name in ("grid_in", "z_out", "y_out", "x_in", "x_out")
    )

    places_xc = []
    for step in range(2 * n.nx):
        x = lax.rem(my_x + far_first(step // 2, n.nx), n.nx)
        places_xc.append(2 * x + lax.rem(my_core + 1 - step % 2, 2))

    def each_x_peer(act):
        def row(step, carry):
            y = lax.rem(my_y + far_first(step, n.ny), n.ny) * (2 * n.nx)
            for place in places_xc:
                act(y + place)
            return carry

        lax.fori_loop(0, n.ny - 1, row, 0)
        for place in places_xc[:-1]:
            act(my_y * (2 * n.nx) + place)

    def t_peer(step):
        return lax.rem(ta + far_first(step, n.ta), n.ta)

    barrier = pltpu.get_barrier_semaphore()

    def greet_x(device):
        pl.semaphore_signal(
            barrier, inc=1, device_id={"gx": device, "ta": ta}, device_id_type=mesh_ids
        )

    each_x_peer(greet_x)
    for step in range(n.ta - 1):
        pl.semaphore_signal(
            barrier, inc=1, device_id={"gx": gx, "ta": t_peer(step)}, device_id_type=mesh_ids
        )
    loads = [
        pltpu.make_async_copy(source, target, load_sem.at[at])
        for at, (source, target) in enumerate(
            (
                (tables_hbm, tables),
                (field_hbm, field),
                (local_hbm, local),
                (weight_hbm, weight_in),
                (cotangent_hbm, cotangent),
            )
        )
    ]
    loads[0].start()
    loads[1].start()

    def received(block, index):
        return pltpu.make_async_remote_copy(
            src_ref=block,
            dst_ref=block,
            send_sem=send_sem.at[index],
            recv_sem=recv_sem.at[index],
            device_id={"gx": gx, "ta": ta},
            device_id_type=mesh_ids,
        )

    def all_x(index):
        return received(got_x.at[index // 2, pl.ds(0, (n.gx - 1) * n.tiles), :], index)

    def all_t(index):
        return received(got_t.at[index // 2, :, pl.ds(0, (n.ta - 1) * 4), :], index)

    def of_x(ref, index, device):
        return ref.at[index // 2, pl.ds(pl.multiple_of(4 * device, 4), n.tiles), :]

    def of_t(ref, index, device):
        return ref.at[index // 2, :, pl.ds(pl.multiple_of(4 * device, 4), 4), :]

    def exchange_x(index):
        def send(peer):
            pltpu.make_async_remote_copy(
                src_ref=of_x(sent_x, index, peer),
                dst_ref=of_x(got_x, index, gx),
                send_sem=send_sem.at[index],
                recv_sem=recv_sem.at[index],
                device_id={"gx": peer, "ta": ta},
                device_id_type=mesh_ids,
            ).start()

        each_x_peer(send)
        pltpu.make_async_copy(
            of_x(sent_x, index, gx), of_x(got_x, index, gx), own_sem.at[index]
        ).start()

    def exchange_t(index):
        for step in range(n.ta - 1):
            peer = t_peer(step)
            pltpu.make_async_remote_copy(
                src_ref=of_t(sent_t, index, peer),
                dst_ref=of_t(got_t, index, ta),
                send_sem=send_sem.at[index],
                recv_sem=recv_sem.at[index],
                device_id={"gx": gx, "ta": peer},
                device_id_type=mesh_ids,
            ).start()
        pltpu.make_async_copy(
            of_t(sent_t, index, ta), of_t(got_t, index, ta), own_sem.at[index]
        ).start()

    def arrived_x(index):
        pltpu.make_async_copy(
            of_x(sent_x, index, gx), of_x(got_x, index, gx), own_sem.at[index]
        ).wait()
        all_x(index).wait_recv()

    def arrived_t(index):
        pltpu.make_async_copy(
            of_t(sent_t, index, ta), of_t(got_t, index, ta), own_sem.at[index]
        ).wait()
        all_t(index).wait_recv()

    def mix_local(source, transposed, start, stop):
        def step(at, carry):
            rows = pl.ds(pl.multiple_of(at * 16, 16), 16)
            values = [source[c, rows, :].astype(F32) for c in range(chans)]
            for d in range(chans):
                total = None
                for c in range(chans):
                    scale = local[d, c] if transposed else local[c, d]
                    term = values[c] * scale
                    total = term if total is None else total + term
                mixed_local[d, rows, :] = total
            return carry

        lax.fori_loop(start, stop, step, 0)

    def turn_weights(part):
        def step(c, carry):
            for block in range(n.blocks):
                pairs[KT * block : KT * block + KT, :chans] = weight_in[part * n.blocks + block, c]
            weight[part, c] = pairs[:LANES, :].T[:chans]
            return carry

        pairs[:LANES, :] = jnp.zeros((LANES, LANES), F32)
        lax.fori_loop(0, chans, step, 0)

    def pack(index):
        parts = []
        for source in (y_cos, y_sin):
            high, low = halves(source[...])
            both = jnp.concatenate([high.astype(BF16), low.astype(BF16)], 1)
            out = lax.dot_general(
                grid_in[...], both, (((1,), (1,)), ((), ())), preferred_element_type=F32
            )
            parts.append(out[: 2 * kf] + out[2 * kf :])
        of_cos, of_sin = parts
        real = of_cos[:kf] - of_sin[kf:]
        imag = -(of_sin[:kf] + of_cos[kf:])
        lane = lax.broadcasted_iota(jnp.int32, (kf, LANES), 1)
        for j in range(kf):
            tile = slice((j // n.fper) * LANES, (j // n.fper + 1) * LANES)
            back = (j % n.fper) * STRIDE
            value = jnp.where(
                lane < chans,
                roll(real[:, tile], -back),
                jnp.where(lane < 2 * chans, roll(imag[:, tile], chans - back), 0.0),
            )
            pairs[j * kf : (j + 1) * kf, :] = value
        for q in range(n.tiles):
            total = None
            for r in range(n.per):
                value = roll(pairs[pl.ds(q * n.per + r, n.gx, stride=n.pb), :], r * n.width)
                total = value if total is None else total + value
            sent_x[index // 2, pl.ds(q, n.gx, stride=4), :] = total

    def unpack(index):
        for q in range(n.tiles):
            received_rows = got_x[index // 2, pl.ds(q, n.gx, stride=4), :]
            for r in range(n.per):
                pairs[pl.ds(q * n.per + r, n.gx, stride=n.pb), :] = roll(
                    received_rows, -r * n.width
                )
        lane = lax.broadcasted_iota(jnp.int32, (kf, LANES), 1)
        all_rows = []
        for tile in range(n.ftiles):
            real = jnp.zeros((kf, LANES), F32)
            imag = jnp.zeros((kf, LANES), F32)
            for part in range(n.fper):
                j = tile * n.fper + part
                if j >= kf:
                    continue
                value = pairs[j * kf : (j + 1) * kf, :]
                begin = part * STRIDE
                here = (lane >= begin) & (lane < begin + chans)
                real = jnp.where(here, roll(value, begin), real)
                imag = jnp.where(here, roll(value, begin - chans), imag)
            high, low = halves(jnp.concatenate([real, imag], 0))
            pad = jnp.zeros((LANES - 4 * kf, LANES), F32)
            all_rows.append(jnp.concatenate([high, low, pad], 0).T.astype(BF16))
        rows = jnp.concatenate(all_rows, 0)
        out = dot(jnp.concatenate([rows, rows], 1), z_out[...])
        z_real[...] = out[:, :cells]
        z_imag[...] = out[:, cells:]

    def put_y(first, out):
        out = out[: 2 * kf] + out[2 * kf :]
        for side in range(2):
            rows = pl.ds(first + side, kf, stride=STRIDE)
            columns = slice(side * cells, (side + 1) * cells)
            y_cos[rows, :] = out[:kf, columns]
            y_sin[rows, :] = out[kf:, columns]

    def along_x(table, values):
        pairs_of = [halves(jnp.concatenate([v, times_i(v, chans)], 0)) for v in values]
        both = [jnp.concatenate([high, low], 0).astype(BF16) for high, low in pairs_of]
        out = dot(table[...], jnp.concatenate(both, 1))
        half = out.shape[0] // 2
        out = out[:half] + out[half:]
        return [out[:, q * LANES : (q + 1) * LANES] for q in range(n.tiles)]

    def analysis_x(index):
        values = [got_x[index // 2, pl.ds(q, n.gx, stride=4), :] for q in range(n.tiles)]
        for q, value in enumerate(along_x(x_in, values)):
            sent_t[(index + 1) // 2, q, :, :] = value

    def synthesis_x(index):
        values = [got_t[index // 2, q, :, :] for q in range(n.tiles)]
        for q, value in enumerate(along_x(x_out, values)):
            sent_x[(index + 1) // 2, pl.ds(q, n.gx, stride=4), :] = value

    upper = lax.broadcasted_iota(jnp.int32, (8, LANES), 0) < 4

    def time_table(kind, m, pair, weight_m):
        first, second = (
            kind(2 * math.pi * ((m * t) % n.ta) / n.ta) * factor * weight_m
            for t in (2 * pair, 2 * pair + 1)
        )
        return first if first == second else jnp.where(upper, first, second)

    def time_in(index):
        for q in range(n.tiles):
            steps = [got_t[index // 2, q, 8 * u : 8 * u + 8, :] for u in range(n.ta // 2)]
            for m in range(KT):
                real = imag = None
                for u in range(n.ta // 2):
                    first = steps[u] * time_table(math.cos, m, u, 1.0)
                    second = steps[u] * time_table(math.sin, m, u, 1.0)
                    real = first if real is None else real + first
                    imag = second if imag is None else imag + second
                value = real - times_i(imag, chans)
                value = value[:4] + value[4:]
                for r in range(n.per):
                    stacked[
                        pl.ds((q * n.per + r) * KT + m, 4, stride=n.pb * KT), :
                    ] = roll(value, -r * n.width)

    def time_out(index):
        stacked[:LANES, :] = turned[...].T
        for q in range(n.tiles):
            values = []
            for m in range(KT):
                total = None
                for r in range(n.per):
                    rows = pl.ds((q * n.per + r) * KT + m, 4, stride=n.pb * KT)
                    value = roll(stacked[rows, :], r * n.width)
                    total = value if total is None else total + value
                total = jnp.concatenate([total, total], 0)
                values.append((total, times_i(total, chans)))
            for u in range(n.ta // 2):
                total = None
                for m in range(KT):
                    scale = 1.0 if m == 0 else 2.0
                    value = values[m][0] * time_table(math.cos, m, u, scale)
                    value += values[m][1] * time_table(math.sin, m, u, scale)
                    total = value if total is None else total + value
                sent_t[index // 2, q, 8 * u : 8 * u + 8, :] = total

    def grad_weights():
        row = lax.broadcasted_iota(jnp.int32, (8, LANES), 0)
        weights = jnp.where(row % KT == 0, 1.0, 2.0)
        for at in range(0, n.modes, 8):
            rows = slice(at, at + 8)
            ours = spec_rows[rows, :] * weights
            real = grad_rows[rows, :]
            imag = roll(real, -chans)
            real, imag = real[:, :chans], imag[:, :chans]
            for c in range(chans):
                spec_r = jnp.broadcast_to(ours[:, c : c + 1], (8, chans))
                spec_i = jnp.broadcast_to(ours[:, chans + c : chans + c + 1], (8, chans))
                out_r = spec_r * real + spec_i * imag
                out_i = spec_r * imag - spec_i * real
                for part in range(2):
                    block = at // KT + part
                    if block < n.blocks:
                        cut = slice(KT * part, KT * part + KT)
                        grad_out[block, c] = out_r[cut]
                        grad_out[n.blocks + block, c] = out_i[cut]

    def analyse_field(pair, carry):
        put_y(2 * pair, dot(grid_in[:, :cells], side_by_side(field, 2 * pair)))
        return carry

    loads[0].wait()
    loads[1].wait()
    for load in loads[2:]:
        load.start()
    lax.fori_loop(0, chans // 2, analyse_field, 0, unroll=5)
    pack(0)
    pl.semaphore_wait(barrier, n.gx - 1 + n.ta - 1)
    exchange_x(0)
    stacked[...] = jnp.zeros_like(stacked)
    turned[...] = jnp.zeros_like(turned)
    loads[3].wait()
    turn_weights(0)
    turn_weights(1)
    loads[2].wait()
    arrived_x(0)
    analysis_x(0)
    exchange_t(1)
    chunks = cells // 16
    mix_local(field, False, 0, 3 * chunks // 8)
    arrived_t(1)
    time_in(1)
    spec[...] = stacked[:LANES, :].T[: n.width]
    real = jnp.zeros((chans, LANES), F32)
    imag = jnp.zeros((chans, LANES), F32)
    for c in range(chans):
        spec_r, spec_i = spec[c : c + 1, :], spec[chans + c : chans + c + 1, :]
        real += spec_r * weight[0, c] - spec_i * weight[1, c]
        imag += spec_r * weight[1, c] + spec_i * weight[0, c]
    turned[:chans, :] = real
    turned[chans : 2 * chans, :] = imag
    spec_rows[...] = stacked[:LANES, :]
    time_out(2)
    exchange_t(2)
    mix_local(field, False, 3 * chunks // 8, 5 * chunks // 8)
    arrived_t(2)
    synthesis_x(2)
    exchange_x(3)
    mix_local(field, False, 5 * chunks // 8, chunks)
    loads[4].wait()
    arrived_x(3)
    unpack(3)

    def activate(pair, carry):
        first = 2 * pair
        pre_act = side_by_side(mixed_local, first) + synthesis(n, y_out, z_real, z_imag, first)
        normal_cdf = 0.5 * (1.0 + lax.erf(pre_act * (1.0 / math.sqrt(2.0))))
        density = jnp.exp(-0.5 * pre_act * pre_act) * (1.0 / math.sqrt(2.0 * math.pi))
        out = pre_act * normal_cdf
        value = side_by_side(cotangent, first).astype(F32) * (normal_cdf + pre_act * density)
        for side in range(2):
            columns = slice(side * cells, (side + 1) * cells)
            layer_out[first + side] = out[:, columns]
            upstream[first + side] = value[:, columns]
        high, low = halves(value)
        put_y(first, dot(grid_in[...], jnp.concatenate([high, low], 0).astype(BF16)))
        return carry

    lax.fori_loop(0, chans // 2, activate, 0, unroll=5)
    pack(4)
    exchange_x(4)
    mix_local(upstream, True, 0, chunks // 2)
    arrived_x(4)
    analysis_x(4)
    exchange_t(5)
    mix_local(upstream, True, chunks // 2, 3 * chunks // 4)
    arrived_t(5)
    time_in(5)
    grad_rows[...] = stacked[:LANES, :]
    spec[...] = stacked[:LANES, :].T[: n.width]
    grad_r, grad_i = spec[:chans, :], spec[chans : 2 * chans, :]
    for c in range(chans):
        turned[c : c + 1, :] = jnp.sum(
            weight[0, c] * grad_r + weight[1, c] * grad_i, 0, keepdims=True
        )
        turned[chans + c : chans + c + 1, :] = jnp.sum(
            weight[0, c] * grad_i - weight[1, c] * grad_r, 0, keepdims=True
        )
    time_out(6)
    exchange_t(6)
    mix_local(upstream, True, 3 * chunks // 4, chunks)
    arrived_t(6)
    synthesis_x(6)
    exchange_x(7)
    grad_weights()
    arrived_x(7)
    unpack(7)
    for index in range(8):
        (all_x if index in (0, 3, 4, 7) else all_t)(index).wait_send()


def finish(
    n,
    layer_in,
    mixed_local,
    z_real,
    z_imag,
    grad_in,
    y_out,
    layer_out,
    grad_field,
    grad_spectral,
    planes,
    sems,
):
    pieces = []
    for source, target in ((grad_in, grad_spectral), (layer_in, layer_out)):
        count = source.shape[0] // PIECES
        for piece in range(PIECES):
            begin = piece * count
            end = begin + count if piece < PIECES - 1 else source.shape[0]
            part = pl.ds(begin, end - begin)
            pieces.append(
                pltpu.make_async_copy(source.at[part], target.at[part], sems.at[1 + len(pieces)])
            )
    for copy in pieces:
        copy.start()

    def step(pair, carry):
        first = 2 * pair
        value = side_by_side(mixed_local, first) + synthesis(n, y_out, z_real, z_imag, first)
        for side in range(2):
            planes[first + side] = value[:, side * n.cells : (side + 1) * n.cells]
        two = pl.ds(first, 2)
        pltpu.make_async_copy(planes.at[two], grad_field.at[two], sems.at[0]).start()
        return carry

    lax.fori_loop(0, n.chans // 2, step, 0, unroll=5)
    for copy in pieces:
        copy.wait()
    pltpu.make_async_copy(planes, grad_field, sems.at[0]).wait()


def shards(n, factor, field, spectral_weight, local_weight, cotangent):
    chans, cells = n.chans, n.cells
    tables, places = make_tables(n)
    weight = jnp.transpose(spectral_weight, (0, 1, 2, 4, 3, 5))
    weight = weight.reshape(2 * n.blocks, chans, KT, chans)
    vmem = pl.BlockSpec(memory_space=pltpu.VMEM)
    hbm = pl.BlockSpec(memory_space=pltpu.HBM)
    wide = jax.ShapeDtypeStruct((chans, cells, cells), F32)
    halfway = jax.ShapeDtypeStruct((n.frows, cells), F32)
    weights = jax.ShapeDtypeStruct(weight.shape, F32)
    rows = max(n.kf * n.kf, LANES)
    results = pl.pallas_call(
        functools.partial(kernel, n, factor, places),
        out_shape=(wide, wide, halfway, halfway, weights),
        in_specs=[hbm] * 5,
        out_specs=(vmem,) * 5,
        scratch_shapes=[
            pltpu.VMEM((chans, cells, cells), BF16),
            pltpu.VMEM((chans, cells, cells), BF16),
            pltpu.VMEM(weight.shape, F32),
            pltpu.SMEM((chans, chans), F32),
            pltpu.VMEM(tables.shape, BF16),
            pltpu.VMEM((2, chans, chans, LANES), F32),
            pltpu.VMEM((chans, cells, cells), F32),
            pltpu.VMEM((n.frows, cells), F32),
            pltpu.VMEM((n.frows, cells), F32),
            pltpu.VMEM((rows, LANES), F32),
            pltpu.VMEM((4 * n.pb * KT, LANES), F32),
            pltpu.VMEM((LANES, LANES), F32),
            pltpu.VMEM((n.width, LANES), F32),
            pltpu.VMEM((LANES, LANES), F32),
            pltpu.VMEM((LANES, LANES), F32),
            pltpu.VMEM((4, 4 * n.gx, LANES), F32),
            pltpu.VMEM((4, 4 * n.gx, LANES), F32),
            pltpu.VMEM((4, n.tiles, n.rows, LANES), F32),
            pltpu.VMEM((4, n.tiles, n.rows, LANES), F32),
            pltpu.SemaphoreType.DMA((5,)),
            pltpu.SemaphoreType.DMA((8,)),
            pltpu.SemaphoreType.DMA((8,)),
            pltpu.SemaphoreType.DMA((8,)),
        ],
        compiler_params=pltpu.CompilerParams(
            collective_id=0, has_side_effects=True, vmem_limit_bytes=40 * 1024 * 1024
        ),
    )(
        *(
            pltpu.with_memory_space_constraint(value, pltpu.HBM)
            for value in (
                field.reshape(chans, cells, cells),
                cotangent.reshape(chans, cells, cells),
                weight,
                local_weight,
                jnp.asarray(tables),
            )
        )
    )
    layer_out, grad_field, grad_spectral = pl.pallas_call(
        functools.partial(finish, n),
        out_shape=(wide, wide, weights),
        in_specs=[vmem] * 6,
        out_specs=(hbm,) * 3,
        scratch_shapes=[
            pltpu.VMEM((chans, cells, cells), F32),
            pltpu.SemaphoreType.DMA((1 + 2 * PIECES,)),
        ],
        compiler_params=pltpu.CompilerParams(vmem_limit_bytes=16 * 1024 * 1024),
    )(*results, jnp.asarray(tables[places["y_out"]]))
    grad_spectral = grad_spectral.reshape(2, n.ib, n.pb, chans, KT, chans)
    grad_spectral = jnp.transpose(grad_spectral, (0, 1, 2, 4, 3, 5))
    return (layer_out.reshape(field.shape), grad_field.reshape(field.shape), grad_spectral)


def solution(mesh, chans=20, kf=24, cells=128):
    n = Sizes(mesh.shape["gx"], mesh.shape["ta"], chans, kf, cells)
    factor = 1.0 / math.sqrt(n.gx * n.ta * cells * cells)
    grid = P(None, "ta", "gx", None, None)
    modes = P(None, "ta", "gx", None, None, None)
    return jax.shard_map(
        functools.partial(shards, n, factor),
        mesh=mesh,
        in_specs=(grid, modes, P(), grid),
        out_specs=(grid, grid, modes),
        check_vma=False,
    )
```

```python
import functools
import math

import jax
import jax.numpy as jnp
import ml_dtypes
import numpy as np
from jax import lax
from jax.experimental import pallas as pl
from jax.experimental.pallas import tpu as pltpu
from jax.sharding import PartitionSpec as P

KT = 4
STRIDE = 32
LANES = 128
F32 = jnp.float32
BF16 = jnp.bfloat16


class Sizes:
    def __init__(self, gx, ta, chans, kf, cells):
        self.gx, self.ta, self.chans, self.kf, self.cells = gx, ta, chans, kf, cells
        self.nx = 4 if gx % 8 == 0 else 1
        self.ny = gx // (2 * self.nx)
        self.pb = kf * kf // gx
        self.ib = kf // ta
        self.width = 2 * chans
        self.per = LANES // self.width
        self.tiles = -(-self.pb // self.per)
        self.rows = 4 * ta
        self.blocks = self.ib * self.pb
        self.modes = self.blocks * KT
        self.fper = LANES // STRIDE
        self.ftiles = -(-kf // self.fper)
        self.frows = self.ftiles * LANES


def split(table):
    table = table.astype(np.float32)
    high = table.astype(ml_dtypes.bfloat16)
    low = (table - high.astype(np.float32)).astype(ml_dtypes.bfloat16)
    return high, low


def two_terms(table):
    high, low = split(table)
    return np.concatenate(
        [np.concatenate([high, high], 1), np.concatenate([low, np.zeros_like(low)], 1)], 0
    )


def make_tables(n):
    half = n.kf // 2
    freq = np.where(np.arange(n.kf) < half, np.arange(n.kf), np.arange(n.kf) - n.kf)
    angle = 2 * np.pi * ((np.arange(n.cells)[:, None] * freq[None, :]) % n.cells) / n.cells
    cos, sin = np.cos(angle), np.sin(angle)
    grid_in = two_terms(np.concatenate([cos.T, sin.T], 0))
    along_z = np.concatenate(
        [np.concatenate([cos.T, sin.T], 1), np.concatenate([-sin.T, cos.T], 1)], 0
    )
    high, low = split(along_z)
    z_out = np.zeros((2 * LANES, 2 * n.cells), ml_dtypes.bfloat16)
    z_out[: 2 * n.kf] = high
    z_out[2 * n.kf : 4 * n.kf] = high
    z_out[LANES : LANES + 2 * n.kf] = low
    high, low = split(np.concatenate([cos, -sin], 1))
    y_out = np.concatenate([high, high, low], 1)
    place = np.arange(n.gx)
    freq_rows = np.zeros((n.rows,), np.int64)
    used = np.zeros((n.rows,), np.float64)
    for block in range(n.ta):
        for i in range(n.ib):
            freq_rows[4 * block + i] = freq[block * n.ib + i]
            used[4 * block + i] = 1.0
    angle = 2 * np.pi * ((freq_rows[:, None] * place[None, :]) % n.gx) / n.gx
    x_in = two_terms(np.concatenate([np.cos(angle), -np.sin(angle)], 1) * used[:, None])
    angle = angle.T
    x_out = two_terms(np.concatenate([np.cos(angle) * used, np.sin(angle) * used], 1))
    places, parts, begin = {}, [], 0
    for name, part in (
        ("grid_in", grid_in),
        ("z_out", z_out),
        ("y_out", y_out),
        ("x_in", x_in),
        ("x_out", x_out),
    ):
        rows = -(-part.shape[0] // 16) * 16
        padded = np.zeros((rows, 256), ml_dtypes.bfloat16)
        padded[: part.shape[0], : part.shape[1]] = part
        places[name] = (slice(begin, begin + part.shape[0]), slice(0, part.shape[1]))
        parts.append(padded)
        begin += rows
    return np.concatenate(parts, 0), places


def halves(value):
    high = value.astype(BF16).astype(F32)
    return high, value - high


def dot(left, right):
    return jnp.dot(left, right, preferred_element_type=F32)


def roll(value, amount):
    amount = amount % LANES
    return value if amount == 0 else pltpu.roll(value, amount, 1)


def times_i(value, chans):
    lane = lax.broadcasted_iota(jnp.int32, value.shape, 1)
    return jnp.where(lane % (2 * chans) < chans, -roll(value, -chans), roll(value, chans))


def far_first(step, count):
    return count // 2 + (1 - 2 * (step % 2)) * ((step + 1) // 2)


def synthesis(n, y_out, z_real, z_imag, first):
    sides = []
    for d in (first, first + 1):
        rows = pl.ds(d, n.kf, stride=STRIDE)
        sides.append(jnp.concatenate([z_real[rows, :], z_imag[rows, :]], 0))
    high, low = halves(jnp.concatenate(sides, 1))
    return dot(y_out[...], jnp.concatenate([high, low, high], 0).astype(BF16))


def side_by_side(ref, first):
    return jnp.concatenate([ref[first], ref[first + 1]], 1)


def kernel(
    n,
    factor,
    places,
    field_hbm,
    cotangent_hbm,
    weight_hbm,
    local_hbm,
    tables_hbm,
    layer_out,
    mixed_local,
    z_real,
    z_imag,
    grad_out,
    field,
    cotangent,
    weight_in,
    local,
    tables,
    weight,
    upstream,
    y_cos,
    y_sin,
    pairs,
    stacked,
    turned,
    spec,
    spec_rows,
    grad_rows,
    sent_x,
    got_x,
    sent_t,
    got_t,
    load_sem,
    own_sem,
    send_sem,
    recv_sem,
):
    chans, kf, cells = n.chans, n.kf, n.cells
    gx, ta = lax.axis_index("gx"), lax.axis_index("ta")
    my_y, my_x, my_core = lax.div(gx, 2 * n.nx), lax.rem(lax.div(gx, 2), n.nx), lax.rem(gx, 2)
    mesh_ids = pl.DeviceIdType.MESH
    grid_in, z_out, y_out, x_in, x_out = (
        tables.at[places[name]] for name in ("grid_in", "z_out", "y_out", "x_in", "x_out")
    )

    places_xc = []
    for step in range(2 * n.nx):
        x = lax.rem(my_x + far_first(step // 2, n.nx), n.nx)
        places_xc.append(2 * x + lax.rem(my_core + 1 - step % 2, 2))

    def each_x_peer(act):
        def row(step, carry):
            y = lax.rem(my_y + far_first(step, n.ny), n.ny) * (2 * n.nx)
            for place in places_xc:
                act(y + place)
            return carry

        lax.fori_loop(0, n.ny - 1, row, 0)
        for place in places_xc[:-1]:
            act(my_y * (2 * n.nx) + place)

    def t_peer(step):
        return lax.rem(ta + far_first(step, n.ta), n.ta)

    barrier = pltpu.get_barrier_semaphore()

    def greet_x(device):
        pl.semaphore_signal(
            barrier, inc=1, device_id={"gx": device, "ta": ta}, device_id_type=mesh_ids
        )

    each_x_peer(greet_x)
    for step in range(n.ta - 1):
        pl.semaphore_signal(
            barrier, inc=1, device_id={"gx": gx, "ta": t_peer(step)}, device_id_type=mesh_ids
        )
    loads = [
        pltpu.make_async_copy(source, target, load_sem.at[at])
        for at, (source, target) in enumerate(
            (
                (tables_hbm, tables),
                (field_hbm, field),
                (local_hbm, local),
                (weight_hbm, weight_in.at[pl.ds(0, 2 * n.blocks)]),
                (cotangent_hbm, cotangent),
            )
        )
    ]
    loads[0].start()
    loads[1].start()

    def received(block, index):
        return pltpu.make_async_remote_copy(
            src_ref=block,
            dst_ref=block,
            send_sem=send_sem.at[index],
            recv_sem=recv_sem.at[index],
            device_id={"gx": gx, "ta": ta},
            device_id_type=mesh_ids,
        )

    def all_x(index):
        return received(got_x.at[index // 2, pl.ds(0, (n.gx - 1) * n.tiles), :], index)

    def all_t(index):
        return received(got_t.at[index // 2, :, pl.ds(0, (n.ta - 1) * 4), :], index)

    def of_x(ref, index, device):
        return ref.at[index // 2, pl.ds(pl.multiple_of(4 * device, 4), n.tiles), :]

    def of_t(ref, index, device):
        return ref.at[index // 2, :, pl.ds(pl.multiple_of(4 * device, 4), 4), :]

    def exchange_x(index):
        def send(peer):
            pltpu.make_async_remote_copy(
                src_ref=of_x(sent_x, index, peer),
                dst_ref=of_x(got_x, index, gx),
                send_sem=send_sem.at[index],
                recv_sem=recv_sem.at[index],
                device_id={"gx": peer, "ta": ta},
                device_id_type=mesh_ids,
            ).start()

        each_x_peer(send)
        pltpu.make_async_copy(
            of_x(sent_x, index, gx), of_x(got_x, index, gx), own_sem.at[index]
        ).start()

    def exchange_t(index):
        for step in range(n.ta - 1):
            peer = t_peer(step)
            pltpu.make_async_remote_copy(
                src_ref=of_t(sent_t, index, peer),
                dst_ref=of_t(got_t, index, ta),
                send_sem=send_sem.at[index],
                recv_sem=recv_sem.at[index],
                device_id={"gx": gx, "ta": peer},
                device_id_type=mesh_ids,
            ).start()
        pltpu.make_async_copy(
            of_t(sent_t, index, ta), of_t(got_t, index, ta), own_sem.at[index]
        ).start()

    def arrived_x(index):
        pltpu.make_async_copy(
            of_x(sent_x, index, gx), of_x(got_x, index, gx), own_sem.at[index]
        ).wait()
        all_x(index).wait_recv()

    def arrived_t(index):
        pltpu.make_async_copy(
            of_t(sent_t, index, ta), of_t(got_t, index, ta), own_sem.at[index]
        ).wait()
        all_t(index).wait_recv()

    def mix_local(source, transposed, start, stop):
        def step(at, carry):
            rows = pl.ds(pl.multiple_of(at * 16, 16), 16)
            values = [source[c, rows, :].astype(F32) for c in range(chans)]
            for d in range(chans):
                total = None
                for c in range(chans):
                    scale = local[d, c] if transposed else local[c, d]
                    term = values[c] * scale
                    total = term if total is None else total + term
                mixed_local[d, rows, :] = total
            return carry

        lax.fori_loop(start, stop, step, 0)

    def turn_weights(part):
        def step(c, carry):
            for block in range(n.blocks):
                pairs[KT * block : KT * block + KT, :chans] = weight_in[part * n.blocks + block, c]
            weight[part, c] = pairs[:LANES, :].T[:chans]
            return carry

        pairs[:LANES, :] = jnp.zeros((LANES, LANES), F32)
        lax.fori_loop(0, chans, step, 0)

    def pack(index):
        parts = []
        for source in (y_cos, y_sin):
            high, low = halves(source[...])
            both = jnp.concatenate([high.astype(BF16), low.astype(BF16)], 1)
            out = lax.dot_general(
                grid_in[...], both, (((1,), (1,)), ((), ())), preferred_element_type=F32
            )
            parts.append(out[: 2 * kf] + out[2 * kf :])
        of_cos, of_sin = parts
        real = of_cos[:kf] - of_sin[kf:]
        imag = -(of_sin[:kf] + of_cos[kf:])
        lane = lax.broadcasted_iota(jnp.int32, (kf, LANES), 1)
        for j in range(kf):
            tile = slice((j // n.fper) * LANES, (j // n.fper + 1) * LANES)
            back = (j % n.fper) * STRIDE
            value = jnp.where(
                lane < chans,
                roll(real[:, tile], -back),
                jnp.where(lane < 2 * chans, roll(imag[:, tile], chans - back), 0.0),
            )
            pairs[j * kf : (j + 1) * kf, :] = value
        for q in range(n.tiles):
            total = None
            for r in range(n.per):
                value = roll(pairs[pl.ds(q * n.per + r, n.gx, stride=n.pb), :], r * n.width)
                total = value if total is None else total + value
            sent_x[index // 2, pl.ds(q, n.gx, stride=4), :] = total

    def unpack(index):
        for q in range(n.tiles):
            received_rows = got_x[index // 2, pl.ds(q, n.gx, stride=4), :]
            for r in range(n.per):
                pairs[pl.ds(q * n.per + r, n.gx, stride=n.pb), :] = roll(
                    received_rows, -r * n.width
                )
        lane = lax.broadcasted_iota(jnp.int32, (kf, LANES), 1)
        all_rows = []
        for tile in range(n.ftiles):
            real = jnp.zeros((kf, LANES), F32)
            imag = jnp.zeros((kf, LANES), F32)
            for part in range(n.fper):
                j = tile * n.fper + part
                if j >= kf:
                    continue
                value = pairs[j * kf : (j + 1) * kf, :]
                begin = part * STRIDE
                here = (lane >= begin) & (lane < begin + chans)
                real = jnp.where(here, roll(value, begin), real)
                imag = jnp.where(here, roll(value, begin - chans), imag)
            high, low = halves(jnp.concatenate([real, imag], 0))
            pad = jnp.zeros((LANES - 4 * kf, LANES), F32)
            all_rows.append(jnp.concatenate([high, low, pad], 0).T.astype(BF16))
        rows = jnp.concatenate(all_rows, 0)
        out = dot(jnp.concatenate([rows, rows], 1), z_out[...])
        z_real[...] = out[:, :cells]
        z_imag[...] = out[:, cells:]

    def put_y(first, out):
        out = out[: 2 * kf] + out[2 * kf :]
        for side in range(2):
            rows = pl.ds(first + side, kf, stride=STRIDE)
            columns = slice(side * cells, (side + 1) * cells)
            y_cos[rows, :] = out[:kf, columns]
            y_sin[rows, :] = out[kf:, columns]

    def along_x(table, values):
        pairs_of = [halves(jnp.concatenate([v, times_i(v, chans)], 0)) for v in values]
        both = [jnp.concatenate([high, low], 0).astype(BF16) for high, low in pairs_of]
        out = dot(table[...], jnp.concatenate(both, 1))
        half = out.shape[0] // 2
        out = out[:half] + out[half:]
        return [out[:, q * LANES : (q + 1) * LANES] for q in range(n.tiles)]

    def analysis_x(index):
        values = [got_x[index // 2, pl.ds(q, n.gx, stride=4), :] for q in range(n.tiles)]
        for q, value in enumerate(along_x(x_in, values)):
            sent_t[(index + 1) // 2, q, :, :] = value

    def synthesis_x(index):
        values = [got_t[index // 2, q, :, :] for q in range(n.tiles)]
        for q, value in enumerate(along_x(x_out, values)):
            sent_x[(index + 1) // 2, pl.ds(q, n.gx, stride=4), :] = value

    upper = lax.broadcasted_iota(jnp.int32, (8, LANES), 0) < 4

    def time_table(kind, m, pair, weight_m):
        first, second = (
            kind(2 * math.pi * ((m * t) % n.ta) / n.ta) * factor * weight_m
            for t in (2 * pair, 2 * pair + 1)
        )
        return first if first == second else jnp.where(upper, first, second)

    def time_in(index):
        for q in range(n.tiles):
            steps = [got_t[index // 2, q, 8 * u : 8 * u + 8, :] for u in range(n.ta // 2)]
            for m in range(KT):
                real = imag = None
                for u in range(n.ta // 2):
                    first = steps[u] * time_table(math.cos, m, u, 1.0)
                    second = steps[u] * time_table(math.sin, m, u, 1.0)
                    real = first if real is None else real + first
                    imag = second if imag is None else imag + second
                value = real - times_i(imag, chans)
                value = value[:4] + value[4:]
                for r in range(n.per):
                    stacked[
                        pl.ds((q * n.per + r) * KT + m, 4, stride=n.pb * KT), :
                    ] = roll(value, -r * n.width)

    def time_out(index):
        stacked[:LANES, :] = turned[...].T
        for q in range(n.tiles):
            values = []
            for m in range(KT):
                total = None
                for r in range(n.per):
                    rows = pl.ds((q * n.per + r) * KT + m, 4, stride=n.pb * KT)
                    value = roll(stacked[rows, :], r * n.width)
                    total = value if total is None else total + value
                total = jnp.concatenate([total, total], 0)
                values.append((total, times_i(total, chans)))
            for u in range(n.ta // 2):
                total = None
                for m in range(KT):
                    scale = 1.0 if m == 0 else 2.0
                    value = values[m][0] * time_table(math.cos, m, u, scale)
                    value += values[m][1] * time_table(math.sin, m, u, scale)
                    total = value if total is None else total + value
                sent_t[index // 2, q, 8 * u : 8 * u + 8, :] = total

    def grad_weights():
        row = lax.broadcasted_iota(jnp.int32, (8, LANES), 0)
        weights = jnp.where(row % KT == 0, 1.0, 2.0)
        for at in range(0, n.modes, 8):
            rows = slice(at, at + 8)
            ours = spec_rows[rows, :] * weights
            real = grad_rows[rows, :]
            imag = roll(real, -chans)
            real, imag = real[:, :chans], imag[:, :chans]
            for c in range(chans):
                spec_r = jnp.broadcast_to(ours[:, c : c + 1], (8, chans))
                spec_i = jnp.broadcast_to(ours[:, chans + c : chans + c + 1], (8, chans))
                out_r = spec_r * real + spec_i * imag
                out_i = spec_r * imag - spec_i * real
                for part in range(2):
                    block = at // KT + part
                    if block < n.blocks:
                        cut = slice(KT * part, KT * part + KT)
                        grad_out[block, c] = out_r[cut]
                        grad_out[n.blocks + block, c] = out_i[cut]

    def analyse_field(pair, carry):
        put_y(2 * pair, dot(grid_in[:, :cells], side_by_side(field, 2 * pair)))
        return carry

    loads[0].wait()
    loads[1].wait()
    for load in loads[2:]:
        load.start()
    lax.fori_loop(0, chans // 2, analyse_field, 0, unroll=5)
    pack(0)
    pl.semaphore_wait(barrier, n.gx - 1 + n.ta - 1)
    exchange_x(0)
    stacked[...] = jnp.zeros_like(stacked)
    turned[...] = jnp.zeros_like(turned)
    loads[3].wait()
    turn_weights(0)
    turn_weights(1)
    loads[2].wait()
    arrived_x(0)
    analysis_x(0)
    exchange_t(1)
    chunks = cells // 16
    mix_local(field, False, 0, 3 * chunks // 8)
    arrived_t(1)
    time_in(1)
    spec[...] = stacked[:LANES, :].T
    real = jnp.zeros((chans, LANES), F32)
    imag = jnp.zeros((chans, LANES), F32)
    for c in range(chans):
        spec_r, spec_i = spec[c : c + 1, :], spec[chans + c : chans + c + 1, :]
        real += spec_r * weight[0, c] - spec_i * weight[1, c]
        imag += spec_r * weight[1, c] + spec_i * weight[0, c]
    turned[:chans, :] = real
    turned[chans : 2 * chans, :] = imag
    spec_rows[...] = stacked[:LANES, :]
    time_out(2)
    exchange_t(2)
    mix_local(field, False, 3 * chunks // 8, 5 * chunks // 8)
    arrived_t(2)
    synthesis_x(2)
    exchange_x(3)
    mix_local(field, False, 5 * chunks // 8, chunks)
    loads[4].wait()
    arrived_x(3)
    unpack(3)

    def activate(pair, carry):
        first = 2 * pair
        pre_act = side_by_side(mixed_local, first) + synthesis(n, y_out, z_real, z_imag, first)
        normal_cdf = 0.5 * (1.0 + lax.erf(pre_act * (1.0 / math.sqrt(2.0))))
        density = jnp.exp(-0.5 * pre_act * pre_act) * (1.0 / math.sqrt(2.0 * math.pi))
        out = pre_act * normal_cdf
        value = side_by_side(cotangent, first).astype(F32) * (normal_cdf + pre_act * density)
        for side in range(2):
            columns = slice(side * cells, (side + 1) * cells)
            layer_out[first + side] = out[:, columns]
            upstream[first + side] = value[:, columns]
        high, low = halves(value)
        put_y(first, dot(grid_in[...], jnp.concatenate([high, low], 0).astype(BF16)))
        return carry

    lax.fori_loop(0, chans // 2, activate, 0, unroll=5)
    pack(4)
    exchange_x(4)
    mix_local(upstream, True, 0, chunks // 2)
    arrived_x(4)
    analysis_x(4)
    exchange_t(5)
    mix_local(upstream, True, chunks // 2, 3 * chunks // 4)
    arrived_t(5)
    time_in(5)
    grad_rows[...] = stacked[:LANES, :]
    spec[...] = stacked[:LANES, :].T
    grad_r, grad_i = spec[:chans, :], spec[chans : 2 * chans, :]
    for c in range(chans):
        turned[c : c + 1, :] = jnp.sum(
            weight[0, c] * grad_r + weight[1, c] * grad_i, 0, keepdims=True
        )
        turned[chans + c : chans + c + 1, :] = jnp.sum(
            weight[0, c] * grad_i - weight[1, c] * grad_r, 0, keepdims=True
        )
    time_out(6)
    exchange_t(6)
    mix_local(upstream, True, 3 * chunks // 4, chunks)
    arrived_t(6)
    synthesis_x(6)
    exchange_x(7)
    grad_weights()
    arrived_x(7)
    unpack(7)
    for index in range(8):
        (all_x if index in (0, 3, 4, 7) else all_t)(index).wait_send()


def finish(
    n,
    layer_in,
    mixed_local,
    z_real,
    z_imag,
    grad_in,
    y_out,
    layer_out,
    grad_field,
    grad_spectral,
    planes,
    sems,
):
    pieces = [
        pltpu.make_async_copy(
            grad_in.at[pl.ds(0, grad_spectral.shape[0])], grad_spectral, sems.at[1]
        ),
        pltpu.make_async_copy(layer_in, layer_out, sems.at[2]),
    ]
    for copy in pieces:
        copy.start()

    def step(pair, carry):
        first = 2 * pair
        value = side_by_side(mixed_local, first) + synthesis(n, y_out, z_real, z_imag, first)
        for side in range(2):
            planes[first + side] = value[:, side * n.cells : (side + 1) * n.cells]
        two = pl.ds(first, 2)
        pltpu.make_async_copy(planes.at[two], grad_field.at[two], sems.at[0]).start()
        return carry

    lax.fori_loop(0, n.chans // 2, step, 0, unroll=5)
    for copy in pieces:
        copy.wait()
    pltpu.make_async_copy(planes, grad_field, sems.at[0]).wait()


def shards(n, factor, field, spectral_weight, local_weight, cotangent):
    chans, cells = n.chans, n.cells
    tables, places = make_tables(n)
    weight = jnp.transpose(spectral_weight, (0, 1, 2, 4, 3, 5))
    weight = weight.reshape(2 * n.blocks, chans, KT, chans)
    vmem = pl.BlockSpec(memory_space=pltpu.VMEM)
    hbm = pl.BlockSpec(memory_space=pltpu.HBM)
    wide = jax.ShapeDtypeStruct((chans, cells, cells), F32)
    halfway = jax.ShapeDtypeStruct((n.frows, cells), F32)
    weights = jax.ShapeDtypeStruct(weight.shape, F32)
    roomy = (weight.shape[0] + 1,) + weight.shape[1:]
    rows = max(n.kf * n.kf, LANES)
    results = pl.pallas_call(
        functools.partial(kernel, n, factor, places),
        out_shape=(wide, wide, halfway, halfway, jax.ShapeDtypeStruct(roomy, F32)),
        in_specs=[hbm] * 5,
        out_specs=(vmem,) * 5,
        scratch_shapes=[
            pltpu.VMEM((chans, cells, cells), BF16),
            pltpu.VMEM((chans, cells, cells), BF16),
            pltpu.VMEM(roomy, F32),
            pltpu.SMEM((chans, chans), F32),
            pltpu.VMEM(tables.shape, BF16),
            pltpu.VMEM((2, chans, chans, LANES), F32),
            pltpu.VMEM((chans, cells, cells), F32),
            pltpu.VMEM((n.frows, cells), F32),
            pltpu.VMEM((n.frows, cells), F32),
            pltpu.VMEM((rows, LANES), F32),
            pltpu.VMEM((8 * n.pb * KT, LANES), F32),
            pltpu.VMEM((LANES, LANES), F32),
            pltpu.VMEM((LANES, LANES), F32),
            pltpu.VMEM((LANES, LANES), F32),
            pltpu.VMEM((LANES, LANES), F32),
            pltpu.VMEM((4, 4 * n.gx, LANES), F32),
            pltpu.VMEM((4, 4 * n.gx, LANES), F32),
            pltpu.VMEM((4, n.tiles, n.rows, LANES), F32),
            pltpu.VMEM((4, n.tiles, n.rows, LANES), F32),
            pltpu.SemaphoreType.DMA((5,)),
            pltpu.SemaphoreType.DMA((8,)),
            pltpu.SemaphoreType.DMA((8,)),
            pltpu.SemaphoreType.DMA((8,)),
        ],
        compiler_params=pltpu.CompilerParams(
            collective_id=0, has_side_effects=True, vmem_limit_bytes=40 * 1024 * 1024
        ),
    )(
        *(
            pltpu.with_memory_space_constraint(value, pltpu.HBM)
            for value in (
                field.reshape(chans, cells, cells),
                cotangent.reshape(chans, cells, cells),
                weight,
                local_weight,
                jnp.asarray(tables),
            )
        )
    )
    layer_out, grad_field, grad_spectral = pl.pallas_call(
        functools.partial(finish, n),
        out_shape=(wide, wide, weights),
        in_specs=[vmem] * 6,
        out_specs=(hbm,) * 3,
        scratch_shapes=[
            pltpu.VMEM((chans, cells, cells), F32),
            pltpu.SemaphoreType.DMA((3,)),
        ],
        compiler_params=pltpu.CompilerParams(vmem_limit_bytes=16 * 1024 * 1024),
    )(*results, jnp.asarray(tables[places["y_out"]]))
    grad_spectral = grad_spectral.reshape(2, n.ib, n.pb, chans, KT, chans)
    grad_spectral = jnp.transpose(grad_spectral, (0, 1, 2, 4, 3, 5))
    return (layer_out.reshape(field.shape), grad_field.reshape(field.shape), grad_spectral)


def solution(mesh, chans=20, kf=24, cells=128):
    n = Sizes(mesh.shape["gx"], mesh.shape["ta"], chans, kf, cells)
    factor = 1.0 / math.sqrt(n.gx * n.ta * cells * cells)
    grid = P(None, "ta", "gx", None, None)
    modes = P(None, "ta", "gx", None, None, None)
    return jax.shard_map(
        functools.partial(shards, n, factor),
        mesh=mesh,
        in_specs=(grid, modes, P(), grid),
        out_specs=(grid, grid, modes),
        check_vma=False,
    )
```

```python
import functools
import math

import jax
import jax.numpy as jnp
import ml_dtypes
import numpy as np
from jax import lax
from jax.experimental import pallas as pl
from jax.experimental.pallas import tpu as pltpu
from jax.sharding import PartitionSpec as P

KT = 4
STRIDE = 32
LANES = 128
F32 = jnp.float32
BF16 = jnp.bfloat16


class Sizes:
    def __init__(self, gx, ta, chans, kf, cells):
        self.gx, self.ta, self.chans, self.kf, self.cells = gx, ta, chans, kf, cells
        self.nx = 4 if gx % 8 == 0 else 1
        self.ny = gx // (2 * self.nx)
        self.pb = kf * kf // gx
        self.ib = kf // ta
        self.width = 2 * chans
        self.per = LANES // self.width
        self.tiles = -(-self.pb // self.per)
        self.rows = 4 * ta
        self.blocks = self.ib * self.pb
        self.modes = self.blocks * KT
        self.fper = LANES // STRIDE
        self.ftiles = -(-kf // self.fper)
        self.frows = self.ftiles * LANES


def split(table):
    table = table.astype(np.float32)
    high = table.astype(ml_dtypes.bfloat16)
    low = (table - high.astype(np.float32)).astype(ml_dtypes.bfloat16)
    return high, low


def two_terms(table):
    high, low = split(table)
    return np.concatenate(
        [np.concatenate([high, high], 1), np.concatenate([low, np.zeros_like(low)], 1)], 0
    )


def make_tables(n):
    half = n.kf // 2
    freq = np.where(np.arange(n.kf) < half, np.arange(n.kf), np.arange(n.kf) - n.kf)
    angle = 2 * np.pi * ((np.arange(n.cells)[:, None] * freq[None, :]) % n.cells) / n.cells
    cos, sin = np.cos(angle), np.sin(angle)
    grid_in = two_terms(np.concatenate([cos.T, sin.T], 0))
    along_z = np.concatenate(
        [np.concatenate([cos.T, sin.T], 1), np.concatenate([-sin.T, cos.T], 1)], 0
    )
    high, low = split(along_z)
    z_out = np.zeros((2 * LANES, 2 * n.cells), ml_dtypes.bfloat16)
    z_out[: 2 * n.kf] = high
    z_out[2 * n.kf : 4 * n.kf] = high
    z_out[LANES : LANES + 2 * n.kf] = low
    high, low = split(np.concatenate([cos, -sin], 1))
    y_out = np.concatenate([high, high, low], 1)
    place = np.arange(n.gx)
    freq_rows = np.zeros((n.rows,), np.int64)
    used = np.zeros((n.rows,), np.float64)
    for block in range(n.ta):
        for i in range(n.ib):
            freq_rows[4 * block + i] = freq[block * n.ib + i]
            used[4 * block + i] = 1.0
    angle = 2 * np.pi * ((freq_rows[:, None] * place[None, :]) % n.gx) / n.gx
    x_in = two_terms(np.concatenate([np.cos(angle), -np.sin(angle)], 1) * used[:, None])
    angle = angle.T
    x_out = two_terms(np.concatenate([np.cos(angle) * used, np.sin(angle) * used], 1))
    places, parts, begin = {}, [], 0
    for name, part in (
        ("grid_in", grid_in),
        ("z_out", z_out),
        ("y_out", y_out),
        ("x_in", x_in),
        ("x_out", x_out),
    ):
        rows = -(-part.shape[0] // 16) * 16
        padded = np.zeros((rows, 256), ml_dtypes.bfloat16)
        padded[: part.shape[0], : part.shape[1]] = part
        places[name] = (slice(begin, begin + part.shape[0]), slice(0, part.shape[1]))
        parts.append(padded)
        begin += rows
    return np.concatenate(parts, 0), places


def halves(value):
    high = value.astype(BF16).astype(F32)
    return high, value - high


def dot(left, right):
    return jnp.dot(left, right, preferred_element_type=F32)


def roll(value, amount):
    amount = amount % LANES
    return value if amount == 0 else pltpu.roll(value, amount, 1)


def times_i(value, chans):
    lane = lax.broadcasted_iota(jnp.int32, value.shape, 1)
    real = lane < chans
    for begin in range(2 * chans, LANES, 2 * chans):
        real = real | ((lane >= begin) & (lane < begin + chans))
    return jnp.where(real, -roll(value, -chans), roll(value, chans))


def far_first(step, count):
    return count // 2 + (1 - 2 * (step % 2)) * ((step + 1) // 2)


def synthesis(n, y_out, z_real, z_imag, first):
    sides = []
    for d in (first, first + 1):
        rows = pl.ds(d, n.kf, stride=STRIDE)
        sides.append(jnp.concatenate([z_real[rows, :], z_imag[rows, :]], 0))
    high, low = halves(jnp.concatenate(sides, 1))
    return dot(y_out[...], jnp.concatenate([high, low, high], 0).astype(BF16))


def side_by_side(ref, first):
    return jnp.concatenate([ref[first], ref[first + 1]], 1)


def kernel(
    n,
    factor,
    places,
    field_hbm,
    cotangent_hbm,
    weight_hbm,
    local_hbm,
    tables_hbm,
    layer_out,
    mixed_local,
    z_real,
    z_imag,
    grad_out,
    field,
    cotangent,
    weight_in,
    local,
    tables,
    weight,
    upstream,
    y_cos,
    y_sin,
    pairs,
    stacked,
    turned,
    spec,
    spec_rows,
    grad_rows,
    sent_x,
    got_x,
    sent_t,
    got_t,
    load_sem,
    own_sem,
    send_sem,
    recv_sem,
):
    chans, kf, cells = n.chans, n.kf, n.cells
    gx, ta = lax.axis_index("gx"), lax.axis_index("ta")
    my_y, my_x, my_core = lax.div(gx, 2 * n.nx), lax.rem(lax.div(gx, 2), n.nx), lax.rem(gx, 2)
    mesh_ids = pl.DeviceIdType.MESH
    grid_in, z_out, y_out, x_in, x_out = (
        tables.at[places[name]] for name in ("grid_in", "z_out", "y_out", "x_in", "x_out")
    )

    places_xc = []
    for step in range(2 * n.nx):
        x = lax.rem(my_x + far_first(step // 2, n.nx), n.nx)
        places_xc.append(2 * x + lax.rem(my_core + 1 - step % 2, 2))

    def each_x_peer(act):
        def row(step, carry):
            y = lax.rem(my_y + far_first(step, n.ny), n.ny) * (2 * n.nx)
            for place in places_xc:
                act(y + place)
            return carry

        lax.fori_loop(0, n.ny - 1, row, 0)
        for place in places_xc[:-1]:
            act(my_y * (2 * n.nx) + place)

    def t_peer(step):
        return lax.rem(ta + far_first(step, n.ta), n.ta)

    barrier = pltpu.get_barrier_semaphore()

    def greet_x(device):
        pl.semaphore_signal(
            barrier, inc=1, device_id={"gx": device, "ta": ta}, device_id_type=mesh_ids
        )

    each_x_peer(greet_x)
    for step in range(n.ta - 1):
        pl.semaphore_signal(
            barrier, inc=1, device_id={"gx": gx, "ta": t_peer(step)}, device_id_type=mesh_ids
        )
    loads = [
        pltpu.make_async_copy(source, target, load_sem.at[at])
        for at, (source, target) in enumerate(
            (
                (tables_hbm, tables),
                (field_hbm, field),
                (local_hbm, local),
                (weight_hbm, weight_in.at[pl.ds(0, 2 * n.blocks)]),
                (cotangent_hbm, cotangent),
            )
        )
    ]
    loads[0].start()
    loads[1].start()

    def received(block, index):
        return pltpu.make_async_remote_copy(
            src_ref=block,
            dst_ref=block,
            send_sem=send_sem.at[index],
            recv_sem=recv_sem.at[index],
            device_id={"gx": gx, "ta": ta},
            device_id_type=mesh_ids,
        )

    def all_x(index):
        return received(got_x.at[index // 2, pl.ds(0, (n.gx - 1) * n.tiles), :], index)

    def all_t(index):
        return received(got_t.at[index // 2, :, pl.ds(0, (n.ta - 1) * 4), :], index)

    def of_x(ref, index, device):
        return ref.at[index // 2, pl.ds(pl.multiple_of(4 * device, 4), n.tiles), :]

    def of_t(ref, index, device):
        return ref.at[index // 2, :, pl.ds(pl.multiple_of(4 * device, 4), 4), :]

    def exchange_x(index):
        def send(peer):
            pltpu.make_async_remote_copy(
                src_ref=of_x(sent_x, index, peer),
                dst_ref=of_x(got_x, index, gx),
                send_sem=send_sem.at[index],
                recv_sem=recv_sem.at[index],
                device_id={"gx": peer, "ta": ta},
                device_id_type=mesh_ids,
            ).start()

        each_x_peer(send)
        pltpu.make_async_copy(
            of_x(sent_x, index, gx), of_x(got_x, index, gx), own_sem.at[index]
        ).start()

    def exchange_t(index):
        for step in range(n.ta - 1):
            peer = t_peer(step)
            pltpu.make_async_remote_copy(
                src_ref=of_t(sent_t, index, peer),
                dst_ref=of_t(got_t, index, ta),
                send_sem=send_sem.at[index],
                recv_sem=recv_sem.at[index],
                device_id={"gx": gx, "ta": peer},
                device_id_type=mesh_ids,
            ).start()
        pltpu.make_async_copy(
            of_t(sent_t, index, ta), of_t(got_t, index, ta), own_sem.at[index]
        ).start()

    def arrived_x(index):
        pltpu.make_async_copy(
            of_x(sent_x, index, gx), of_x(got_x, index, gx), own_sem.at[index]
        ).wait()
        all_x(index).wait_recv()

    def arrived_t(index):
        pltpu.make_async_copy(
            of_t(sent_t, index, ta), of_t(got_t, index, ta), own_sem.at[index]
        ).wait()
        all_t(index).wait_recv()

    def mix_local(source, transposed, start, stop):
        def step(at, carry):
            rows = pl.ds(pl.multiple_of(at * 16, 16), 16)
            values = [source[c, rows, :].astype(F32) for c in range(chans)]
            for d in range(chans):
                total = None
                for c in range(chans):
                    scale = local[d, c] if transposed else local[c, d]
                    term = values[c] * scale
                    total = term if total is None else total + term
                mixed_local[d, rows, :] = total
            return carry

        lax.fori_loop(start, stop, step, 0)

    def turn_weights(part):
        def step(c, carry):
            for block in range(n.blocks):
                pairs[KT * block : KT * block + KT, :chans] = weight_in[part * n.blocks + block, c]
            weight[part, c] = pairs[:LANES, :].T[:chans]
            return carry

        pairs[:LANES, :] = jnp.zeros((LANES, LANES), F32)
        lax.fori_loop(0, chans, step, 0)

    def pack(index):
        parts = []
        for source in (y_cos, y_sin):
            high, low = halves(source[...])
            both = jnp.concatenate([high.astype(BF16), low.astype(BF16)], 1)
            out = lax.dot_general(
                grid_in[...], both, (((1,), (1,)), ((), ())), preferred_element_type=F32
            )
            parts.append(out[: 2 * kf] + out[2 * kf :])
        of_cos, of_sin = parts
        real = of_cos[:kf] - of_sin[kf:]
        imag = -(of_sin[:kf] + of_cos[kf:])
        lane = lax.broadcasted_iota(jnp.int32, (kf, LANES), 1)
        for j in range(kf):
            tile = slice((j // n.fper) * LANES, (j // n.fper + 1) * LANES)
            begin = (j % n.fper) * STRIDE
            if begin == 0:
                beside = roll(imag[:, tile], chans)
            here = (lane >= begin) & (lane < begin + chans)
            value = roll(jnp.where(here, real[:, tile], beside), -begin)
            pairs[j * kf : (j + 1) * kf, :] = jnp.where(lane < 2 * chans, value, 0.0)
        for q in range(n.tiles):
            total = None
            for r in range(n.per):
                value = roll(pairs[pl.ds(q * n.per + r, n.gx, stride=n.pb), :], r * n.width)
                total = value if total is None else total + value
            sent_x[index // 2, pl.ds(q, n.gx, stride=4), :] = total

    def unpack(index):
        for q in range(n.tiles):
            received_rows = got_x[index // 2, pl.ds(q, n.gx, stride=4), :]
            for r in range(n.per):
                pairs[pl.ds(q * n.per + r, n.gx, stride=n.pb), :] = roll(
                    received_rows, -r * n.width
                )
        lane = lax.broadcasted_iota(jnp.int32, (kf, LANES), 1)
        all_rows = []
        for tile in range(n.ftiles):
            real = jnp.zeros((kf, LANES), F32)
            imag = jnp.zeros((kf, LANES), F32)
            for part in range(n.fper):
                j = tile * n.fper + part
                if j >= kf:
                    continue
                value = pairs[j * kf : (j + 1) * kf, :]
                begin = part * STRIDE
                value = roll(value, begin)
                real = jnp.where((lane >= begin) & (lane < begin + chans), value, real)
                first = (begin + chans) % LANES
                last = (begin + 2 * chans) % LANES
                if first < last:
                    beside = (lane >= first) & (lane < last)
                else:
                    beside = (lane >= first) | (lane < last)
                imag = jnp.where(beside, value, imag)
            imag = roll(imag, -chans)
            high, low = halves(jnp.concatenate([real, imag], 0))
            pad = jnp.zeros((LANES - 4 * kf, LANES), F32)
            all_rows.append(jnp.concatenate([high, low, pad], 0).T.astype(BF16))
        rows = jnp.concatenate(all_rows, 0)
        out = dot(jnp.concatenate([rows, rows], 1), z_out[...])
        z_real[...] = out[:, :cells]
        z_imag[...] = out[:, cells:]

    def put_y(first, out):
        out = out[: 2 * kf] + out[2 * kf :]
        for side in range(2):
            rows = pl.ds(first + side, kf, stride=STRIDE)
            columns = slice(side * cells, (side + 1) * cells)
            y_cos[rows, :] = out[:kf, columns]
            y_sin[rows, :] = out[kf:, columns]

    def along_x(table, values):
        pairs_of = [halves(jnp.concatenate([v, times_i(v, chans)], 0)) for v in values]
        both = [jnp.concatenate([high, low], 0).astype(BF16) for high, low in pairs_of]
        out = dot(table[...], jnp.concatenate(both, 1))
        half = out.shape[0] // 2
        out = out[:half] + out[half:]
        return [out[:, q * LANES : (q + 1) * LANES] for q in range(n.tiles)]

    def analysis_x(index):
        values = [got_x[index // 2, pl.ds(q, n.gx, stride=4), :] for q in range(n.tiles)]
        for q, value in enumerate(along_x(x_in, values)):
            sent_t[(index + 1) // 2, q, :, :] = value

    def synthesis_x(index):
        values = [got_t[index // 2, q, :, :] for q in range(n.tiles)]
        for q, value in enumerate(along_x(x_out, values)):
            sent_x[(index + 1) // 2, pl.ds(q, n.gx, stride=4), :] = value

    upper = lax.broadcasted_iota(jnp.int32, (8, LANES), 0) < 4

    def time_table(kind, m, pair, weight_m):
        first, second = (
            kind(2 * math.pi * ((m * t) % n.ta) / n.ta) * factor * weight_m
            for t in (2 * pair, 2 * pair + 1)
        )
        return first if first == second else jnp.where(upper, first, second)

    def time_in(index):
        for q in range(n.tiles):
            steps = [got_t[index // 2, q, 8 * u : 8 * u + 8, :] for u in range(n.ta // 2)]
            for m in range(KT):
                real = imag = None
                for u in range(n.ta // 2):
                    first = steps[u] * time_table(math.cos, m, u, 1.0)
                    second = steps[u] * time_table(math.sin, m, u, 1.0)
                    real = first if real is None else real + first
                    imag = second if imag is None else imag + second
                value = real - times_i(imag, chans)
                value = value[:4] + value[4:]
                for r in range(n.per):
                    stacked[
                        pl.ds((q * n.per + r) * KT + m, 4, stride=n.pb * KT), :
                    ] = roll(value, -r * n.width)

    def time_out(index):
        stacked[:LANES, :] = turned[...].T
        for q in range(n.tiles):
            values = []
            for m in range(KT):
                total = None
                for r in range(n.per):
                    rows = pl.ds((q * n.per + r) * KT + m, 4, stride=n.pb * KT)
                    value = roll(stacked[rows, :], r * n.width)
                    total = value if total is None else total + value
                total = jnp.concatenate([total, total], 0)
                values.append((total, times_i(total, chans)))
            for u in range(n.ta // 2):
                total = None
                for m in range(KT):
                    scale = 1.0 if m == 0 else 2.0
                    value = values[m][0] * time_table(math.cos, m, u, scale)
                    value += values[m][1] * time_table(math.sin, m, u, scale)
                    total = value if total is None else total + value
                sent_t[index // 2, q, 8 * u : 8 * u + 8, :] = total

    def grad_weights():
        row = lax.broadcasted_iota(jnp.int32, (8, LANES), 0)
        weights = jnp.where(row % KT == 0, 1.0, 2.0)
        for at in range(0, n.modes, 8):
            rows = slice(at, at + 8)
            ours = spec_rows[rows, :] * weights
            real = grad_rows[rows, :]
            imag = roll(real, -chans)
            real, imag = real[:, :chans], imag[:, :chans]
            for c in range(chans):
                spec_r = jnp.broadcast_to(ours[:, c : c + 1], (8, chans))
                spec_i = jnp.broadcast_to(ours[:, chans + c : chans + c + 1], (8, chans))
                out_r = spec_r * real + spec_i * imag
                out_i = spec_r * imag - spec_i * real
                for part in range(2):
                    block = at // KT + part
                    if block < n.blocks:
                        cut = slice(KT * part, KT * part + KT)
                        grad_out[block, c] = out_r[cut]
                        grad_out[n.blocks + block, c] = out_i[cut]

    def analyse_field(pair, carry):
        put_y(2 * pair, dot(grid_in[:, :cells], side_by_side(field, 2 * pair)))
        return carry

    loads[0].wait()
    loads[1].wait()
    for load in loads[2:]:
        load.start()
    lax.fori_loop(0, chans // 2, analyse_field, 0, unroll=5)
    pack(0)
    pl.semaphore_wait(barrier, n.gx - 1 + n.ta - 1)
    exchange_x(0)
    stacked[...] = jnp.zeros_like(stacked)
    turned[...] = jnp.zeros_like(turned)
    loads[3].wait()
    turn_weights(0)
    turn_weights(1)
    loads[2].wait()
    arrived_x(0)
    analysis_x(0)
    exchange_t(1)
    chunks = cells // 16
    mix_local(field, False, 0, 3 * chunks // 8)
    arrived_t(1)
    time_in(1)
    spec[...] = stacked[:LANES, :].T
    real = jnp.zeros((chans, LANES), F32)
    imag = jnp.zeros((chans, LANES), F32)
    for c in range(chans):
        spec_r, spec_i = spec[c : c + 1, :], spec[chans + c : chans + c + 1, :]
        real += spec_r * weight[0, c] - spec_i * weight[1, c]
        imag += spec_r * weight[1, c] + spec_i * weight[0, c]
    turned[:chans, :] = real
    turned[chans : 2 * chans, :] = imag
    spec_rows[...] = stacked[:LANES, :]
    time_out(2)
    exchange_t(2)
    mix_local(field, False, 3 * chunks // 8, 5 * chunks // 8)
    arrived_t(2)
    synthesis_x(2)
    exchange_x(3)
    mix_local(field, False, 5 * chunks // 8, chunks)
    loads[4].wait()
    arrived_x(3)
    unpack(3)

    def activate(pair, carry):
        first = 2 * pair
        pre_act = side_by_side(mixed_local, first) + synthesis(n, y_out, z_real, z_imag, first)
        normal_cdf = 0.5 * (1.0 + lax.erf(pre_act * (1.0 / math.sqrt(2.0))))
        density = jnp.exp(-0.5 * pre_act * pre_act) * (1.0 / math.sqrt(2.0 * math.pi))
        out = pre_act * normal_cdf
        value = side_by_side(cotangent, first).astype(F32) * (normal_cdf + pre_act * density)
        for side in range(2):
            columns = slice(side * cells, (side + 1) * cells)
            layer_out[first + side] = out[:, columns]
            upstream[first + side] = value[:, columns]
        high, low = halves(value)
        put_y(first, dot(grid_in[...], jnp.concatenate([high, low], 0).astype(BF16)))
        return carry

    lax.fori_loop(0, chans // 2, activate, 0, unroll=5)
    pack(4)
    exchange_x(4)
    mix_local(upstream, True, 0, chunks // 2)
    arrived_x(4)
    analysis_x(4)
    exchange_t(5)
    mix_local(upstream, True, chunks // 2, 3 * chunks // 4)
    arrived_t(5)
    time_in(5)
    grad_rows[...] = stacked[:LANES, :]
    spec[...] = stacked[:LANES, :].T
    grad_r, grad_i = spec[:chans, :], spec[chans : 2 * chans, :]
    for c in range(chans):
        turned[c : c + 1, :] = jnp.sum(
            weight[0, c] * grad_r + weight[1, c] * grad_i, 0, keepdims=True
        )
        turned[chans + c : chans + c + 1, :] = jnp.sum(
            weight[0, c] * grad_i - weight[1, c] * grad_r, 0, keepdims=True
        )
    time_out(6)
    exchange_t(6)
    mix_local(upstream, True, 3 * chunks // 4, chunks)
    arrived_t(6)
    synthesis_x(6)
    exchange_x(7)
    grad_weights()
    arrived_x(7)
    unpack(7)
    for index in range(8):
        (all_x if index in (0, 3, 4, 7) else all_t)(index).wait_send()


def finish(
    n,
    layer_in,
    mixed_local,
    z_real,
    z_imag,
    grad_in,
    y_out,
    layer_out,
    grad_field,
    grad_spectral,
    planes,
    sems,
):
    pieces = [
        pltpu.make_async_copy(
            grad_in.at[pl.ds(0, grad_spectral.shape[0])], grad_spectral, sems.at[1]
        ),
        pltpu.make_async_copy(layer_in, layer_out, sems.at[2]),
    ]
    for copy in pieces:
        copy.start()

    def step(pair, carry):
        first = 2 * pair
        value = side_by_side(mixed_local, first) + synthesis(n, y_out, z_real, z_imag, first)
        for side in range(2):
            planes[first + side] = value[:, side * n.cells : (side + 1) * n.cells]
        two = pl.ds(first, 2)
        pltpu.make_async_copy(planes.at[two], grad_field.at[two], sems.at[0]).start()
        return carry

    lax.fori_loop(0, n.chans // 2, step, 0, unroll=5)
    for copy in pieces:
        copy.wait()
    pltpu.make_async_copy(planes, grad_field, sems.at[0]).wait()


def shards(n, factor, field, spectral_weight, local_weight, cotangent):
    chans, cells = n.chans, n.cells
    tables, places = make_tables(n)
    weight = jnp.transpose(spectral_weight, (0, 1, 2, 4, 3, 5))
    weight = weight.reshape(2 * n.blocks, chans, KT, chans)
    vmem = pl.BlockSpec(memory_space=pltpu.VMEM)
    hbm = pl.BlockSpec(memory_space=pltpu.HBM)
    wide = jax.ShapeDtypeStruct((chans, cells, cells), F32)
    halfway = jax.ShapeDtypeStruct((n.frows, cells), F32)
    weights = jax.ShapeDtypeStruct(weight.shape, F32)
    roomy = (weight.shape[0] + 1,) + weight.shape[1:]
    rows = max(n.kf * n.kf, LANES)
    results = pl.pallas_call(
        functools.partial(kernel, n, factor, places),
        out_shape=(wide, wide, halfway, halfway, jax.ShapeDtypeStruct(roomy, F32)),
        in_specs=[hbm] * 5,
        out_specs=(vmem,) * 5,
        scratch_shapes=[
            pltpu.VMEM((chans, cells, cells), BF16),
            pltpu.VMEM((chans, cells, cells), BF16),
            pltpu.VMEM(roomy, F32),
            pltpu.SMEM((chans, chans), F32),
            pltpu.VMEM(tables.shape, BF16),
            pltpu.VMEM((2, chans, chans, LANES), F32),
            pltpu.VMEM((chans, cells, cells), F32),
            pltpu.VMEM((n.frows, cells), F32),
            pltpu.VMEM((n.frows, cells), F32),
            pltpu.VMEM((rows, LANES), F32),
            pltpu.VMEM((8 * n.pb * KT, LANES), F32),
            pltpu.VMEM((LANES, LANES), F32),
            pltpu.VMEM((LANES, LANES), F32),
            pltpu.VMEM((LANES, LANES), F32),
            pltpu.VMEM((LANES, LANES), F32),
            pltpu.VMEM((4, 4 * n.gx, LANES), F32),
            pltpu.VMEM((4, 4 * n.gx, LANES), F32),
            pltpu.VMEM((4, n.tiles, n.rows, LANES), F32),
            pltpu.VMEM((4, n.tiles, n.rows, LANES), F32),
            pltpu.SemaphoreType.DMA((5,)),
            pltpu.SemaphoreType.DMA((8,)),
            pltpu.SemaphoreType.DMA((8,)),
            pltpu.SemaphoreType.DMA((8,)),
        ],
        compiler_params=pltpu.CompilerParams(
            collective_id=0, has_side_effects=True, vmem_limit_bytes=40 * 1024 * 1024
        ),
    )(
        *(
            pltpu.with_memory_space_constraint(value, pltpu.HBM)
            for value in (
                field.reshape(chans, cells, cells),
                cotangent.reshape(chans, cells, cells),
                weight,
                local_weight,
                jnp.asarray(tables),
            )
        )
    )
    layer_out, grad_field, grad_spectral = pl.pallas_call(
        functools.partial(finish, n),
        out_shape=(wide, wide, weights),
        in_specs=[vmem] * 6,
        out_specs=(hbm,) * 3,
        scratch_shapes=[
            pltpu.VMEM((chans, cells, cells), F32),
            pltpu.SemaphoreType.DMA((3,)),
        ],
        compiler_params=pltpu.CompilerParams(vmem_limit_bytes=16 * 1024 * 1024),
    )(*results, jnp.asarray(tables[places["y_out"]]))
    grad_spectral = grad_spectral.reshape(2, n.ib, n.pb, chans, KT, chans)
    grad_spectral = jnp.transpose(grad_spectral, (0, 1, 2, 4, 3, 5))
    return (layer_out.reshape(field.shape), grad_field.reshape(field.shape), grad_spectral)


def solution(mesh, chans=20, kf=24, cells=128):
    n = Sizes(mesh.shape["gx"], mesh.shape["ta"], chans, kf, cells)
    factor = 1.0 / math.sqrt(n.gx * n.ta * cells * cells)
    grid = P(None, "ta", "gx", None, None)
    modes = P(None, "ta", "gx", None, None, None)
    return jax.shard_map(
        functools.partial(shards, n, factor),
        mesh=mesh,
        in_specs=(grid, modes, P(), grid),
        out_specs=(grid, grid, modes),
        check_vma=False,
    )
```
